256 devices in a mesh: gz: 32 (over z_hi, y, core), gy: 8 (over z_lo, x).
Axes of the slice: x: 4, y: 4, z: 8 (z_hi: 4, z_lo: 2; z = z_hi * 2 + z_lo), core: 2. Of those that a mesh axis runs over, the one named last changes fastest.
Arguments:
- raw_planes: bfloat16 [256, 1024, 1024], P('gz', None, 'gy'), may hold values from 0 to 41, as said below
- slot_plane: int32 [256], P('gz'), may hold values from -1 to 127, as said below
- shear_offsets: int32 [128], replicated, may hold values from 0 to 255
- dark_level: float32 [128], replicated, may hold values from 0.2 to 1
- profile_z: float32 [2, 41], replicated, may hold values from 0.005 to 0.05
- profile_x: float32 [2, 15], replicated, may hold values from 0.02 to 0.15
- profile_y: float32 [2, 15], replicated, may hold values from 0.02 to 0.15
Outputs:
- estimate: float32 [128, 1024, 1024], P('gz', None, 'gy')
The draws below stay inside these ranges and needn't reach their ends.
Inputs may be any that keep to these rules, and one draw needn't show every extreme that they name: `slot_plane`: every plane 0 to 127 stands in exactly one slot and a slot without a plane holds -1. The 8 slots of one index of gz hold at most 8 planes, in no fixed slot order, and some index holds exactly 8 in every draw. The planes of one index are consecutive numbers, and higher indices hold higher planes. `raw_planes`: nonnegative camera counts.
All inputs are finite; a program needn't handle non-finite values.
Results may differ from the reference program's by a relative error of at most 0.00055.
Values may be sent and summed in bfloat16 or wider, within the bound.
A program may use at most 128 MiB of HBM per device.

```python
import math
import jax
import jax.numpy as jnp
from jax import lax

X = 1024
Y = 1024
KZ = 41
KX = 15
KY = 15
RANK = 2
ITERS = 2
SHEAR = 256
CAP = 8
S = 128
SLOTS = 256


def spotted_counts(key, base_lo, base_hi, chance, bright_lo, bright_hi):
    key_base, key_mask, key_bright = jax.random.split(key, 3)
    outline = (SLOTS, X, Y)
    background = jax.random.uniform(key_base, outline, jnp.float32, base_lo, base_hi)
    lit = jax.random.uniform(key_mask, outline, jnp.float32) < chance
    level = jax.random.uniform(key_bright, outline, jnp.float32, jnp.log(bright_lo), jnp.log(bright_hi))
    return background + jnp.where(lit, jnp.exp(level), 0.0)


def draw_raw_planes(key, part):
    key = jax.random.fold_in(key, 23)
    values = spotted_counts(key, 0.2, 1.0, 1.0 / 48.0, 2.0, 30.0)
    return values.astype(jnp.bfloat16)


def draw_slot_plane(key, part):
    key = jax.random.fold_in(key, 11)
    devices = SLOTS // CAP
    average = CAP // 2
    key_order, key_moves, key_ranks = jax.random.split(key, 3)
    order = jax.random.permutation(key_order, devices)
    moves = jax.random.randint(key_moves, (devices // 2,), 0, average + 1).astype(jnp.int32)
    moves = moves.at[0].set(average)
    position = jnp.zeros((devices,), jnp.int32).at[order].set(jnp.arange(devices, dtype=jnp.int32))
    paired = position // 2
    signed = 1 - 2 * (position % 2)
    counts = average + signed * moves[paired]
    starts = jnp.cumsum(counts) - counts
    ranks = jax.vmap(lambda one_key: jax.random.permutation(one_key, CAP))(jax.random.split(key_ranks, devices)).astype(jnp.int32)
    planes = jnp.where(ranks < counts[:, None], starts[:, None] + ranks, -1)
    return planes.reshape(-1).astype(jnp.int32)


def place_ends(array, own_key, low, top_value):
    longest = array.shape.index(max(array.shape))
    spots = []
    for shift in (0, 1):
        where = [jax.random.randint(jax.random.fold_in(own_key, axis), (), 0, length) for axis, length in enumerate(array.shape)]
        where[longest] = (where[longest] + shift) % array.shape[longest]
        spots.append(tuple(where))
    return array.at[spots[0]].set(low).at[spots[1]].set(top_value)


def setup_inputs(seed: int = 0) -> dict:
    keys = jax.random.split(jax.random.key(seed), 8)
    return {
        "raw_planes": draw_raw_planes(jax.random.fold_in(keys[7], 71), 0),
        "slot_plane": draw_slot_plane(jax.random.fold_in(keys[7], 71), 0),
        "shear_offsets": place_ends(jax.random.randint(keys[2], (S,), 0, SHEAR), jax.random.fold_in(keys[2], 1), 0, SHEAR - 1).astype(jnp.int32),
        "dark_level": jnp.clip(jnp.exp(jax.random.uniform(keys[3], (S,), jnp.float32, math.log(0.2), math.log(1.0))), 0.2, 1.0),
        "profile_z": jnp.clip(jnp.exp(jax.random.uniform(keys[4], (RANK, KZ), jnp.float32, math.log(0.005), math.log(0.05))), 0.005, 0.05),
        "profile_x": jnp.clip(jnp.exp(jax.random.uniform(keys[5], (RANK, KX), jnp.float32, math.log(0.02), math.log(0.15))), 0.02, 0.15),
        "profile_y": jnp.clip(jnp.exp(jax.random.uniform(keys[6], (RANK, KY), jnp.float32, math.log(0.02), math.log(0.15))), 0.02, 0.15),
    }


def blur_axis(volume, weights, dim_index, mirror):
    extent = weights.shape[0]
    half_width = extent // 2
    kernel = weights[::-1] if mirror else weights
    shifted = jnp.moveaxis(volume, dim_index, -1)
    outline = shifted.shape
    flattened = shifted.reshape(-1, 1, outline[-1])
    result = lax.conv_general_dilated(flattened, kernel.reshape(1, 1, extent), (1,), [(half_width, half_width)], precision=lax.Precision.HIGHEST)
    return jnp.moveaxis(result.reshape(outline), -1, dim_index)


def operator(volume, profile_z, profile_x, profile_y, mirror):
    summed = jnp.zeros_like(volume)
    for component in range(RANK):
        partial_sum = blur_axis(volume, profile_z[component], 0, mirror)
        partial_sum = blur_axis(partial_sum, profile_x[component], 1, mirror)
        partial_sum = blur_axis(partial_sum, profile_y[component], 2, mirror)
        summed = summed + partial_sum
    return summed


def shift_plane(bundle):
    one_plane, offset = bundle
    padded = jnp.pad(one_plane, ((SHEAR, 0), (0, 0)))
    return lax.dynamic_slice_in_dim(padded, (SHEAR - offset).astype(jnp.int32), X, 0)


def reference(raw_planes, slot_plane, shear_offsets, dark_level, profile_z, profile_x, profile_y):
    target = jnp.where(slot_plane >= 0, slot_plane, S).astype(jnp.int32)
    placed = jnp.zeros((S, X, Y), jnp.float32).at[target].set(raw_planes.astype(jnp.float32), mode="drop")
    observed = lax.map(shift_plane, (placed, shear_offsets.astype(jnp.int32)))
    dark_col = dark_level[:, None, None]
    estimate = observed + dark_col
    for iteration in range(ITERS):
        blurred = operator(estimate, profile_z, profile_x, profile_y, True) + dark_col
        quotient = observed / blurred
        estimate = estimate * operator(quotient, profile_z, profile_x, profile_y, False)
    return estimate
```

```python
import jax
import jax.numpy as jnp
from jax import lax
from jax.experimental import pallas as pl
from jax.experimental.pallas import tpu as pltpu
from jax.sharding import PartitionSpec as P

SHEAR = 256
ITERS = 2
NZ = 128
NB = 32
XB = 32
YB = 128
CAP = 8
TX = 15
TZ = 41
MESH = pl.DeviceIdType.MESH
BF = jnp.bfloat16
F32 = jnp.float32
I32 = jnp.int32
V = pl.BlockSpec(memory_space=pltpu.VMEM)
SM = pl.BlockSpec(memory_space=pltpu.SMEM)
ANY = pl.BlockSpec(memory_space=pl.ANY)


def params(mib, **kw):
    return pltpu.CompilerParams(vmem_limit_bytes=mib * 2**20, **kw)


def snake(g):
    high = lax.div(g, 8)
    y = lax.rem(lax.div(g, 2), 4)
    flip = lax.rem(high, 2)
    return high * 8 + (y + flip * (3 - 2 * y)) * 2 + lax.rem(g, 2)


def iota(shape, dim):
    return lax.broadcasted_iota(I32, shape, dim)


def dot(a, b):
    return jnp.dot(a, b, preferred_element_type=F32)


def split(v):
    hi = v.astype(BF)
    return hi, (v - hi.astype(F32)).astype(BF)


def toeplitz(profile, r, distance, extent, mirror):
    total = jnp.zeros(distance.shape, F32)
    for d in range(extent):
        total = jnp.where(distance == d, profile[r, extent - 1 - d if mirror else d], total)
    return total


def tables_kernel(pz, px, py, dark, wy_hi, wy_lo, bz_hl, edges, dark_col):
    for kind in range(2):
        mirror = kind == 0
        for r in range(2):
            lanes = pl.ds(r * 128, 128)
            row = iota((128, 128), 0)
            col = iota((128, 128), 1)
            hi, lo = split(toeplitz(py, r, row - col + 7, TX, mirror))
            for s in range(8):
                wy_hi[kind, s, 0:128, lanes] = hi
                wy_lo[kind, s, 0:128, lanes] = lo
            h = lax.rem(row, 16)
            source = jnp.where(h < 8, h - 7, h + 120)
            distance = jnp.where(lax.rem(h, 8) == 7, -1, source - col + 7)
            halo = toeplitz(py, r, distance, TX, mirror)
            for s in range(8):
                hi, lo = split(jnp.where(lax.div(row, 16) == s, halo, 0.0))
                wy_hi[kind, s, 128:256, lanes] = hi
                wy_lo[kind, s, 128:256, lanes] = lo
            hi, lo = split(toeplitz(pz, r, col - row + TZ // 2, TZ, mirror))
            bz_hl[kind, 0:128, lanes] = hi
            bz_hl[kind, 128:256, lanes] = lo
    row = iota((128, 128), 0)
    col = iota((128, 128), 1)
    for s in range(8):
        near = (col == s * 16 + 8 + row) & (row < 7)
        far = (col == s * 16 + row - 121) & (row >= 121)
        edges[s, :, 0:128] = jnp.where(near, 1.0, 0.0).astype(BF)
        edges[s, :, 128:256] = jnp.where(far, 1.0, 0.0).astype(BF)
    level = jnp.sum(jnp.where(row == col, dark[...], 0.0), axis=1, keepdims=True)
    dark_col[...] = jnp.broadcast_to(level, (128, 128))


def make_tables(profile_z, profile_x, profile_y, dark_level):
    return pl.pallas_call(
        tables_kernel,
        out_shape=[
            jax.ShapeDtypeStruct((2, 8, 256, 256), BF),
            jax.ShapeDtypeStruct((2, 8, 256, 256), BF),
            jax.ShapeDtypeStruct((2, 256, 256), BF),
            jax.ShapeDtypeStruct((8, 128, 256), BF),
            jax.ShapeDtypeStruct((128, 128), F32),
        ],
        in_specs=[SM, SM, SM, V],
        out_specs=[V] * 5,
        compiler_params=params(24),
        name="tables",
    )(profile_z, profile_x, profile_y, dark_level.reshape(1, 128))


def shear_kernel(slot, offsets, raw, blocks, label_row, padded, woven):
    columns = raw.shape[1]
    lane = lax.rem(iota((1, 128), 1), CAP)
    labels = jnp.zeros((1, 128), I32)
    for k in range(2):
        padded[k, 0:SHEAR] = jnp.zeros((SHEAR, 128), F32)
    for c in range(CAP):
        plane = slot[c]
        labels = jnp.where(lane == c, plane, labels)
        start = SHEAR - offsets[jnp.maximum(plane, 0)]
        k = c % 2
        for x in range(0, columns, 256):
            padded[k, SHEAR + x : SHEAR + x + 256] = raw[c, x : x + 256].astype(F32)
        for x in range(0, columns, 256):
            woven[pl.ds(x * CAP + c, 256, stride=CAP), :] = padded[k, pl.ds(start + x, 256), :]
    label_row[...] = labels

    def pack(i, carry):
        at = pl.ds(pl.multiple_of(i * 512, 512), 512)
        blocks[pl.ds(i * 32, 32)] = woven[at, :].reshape(32, 16, 128).astype(BF)
        return carry

    lax.fori_loop(0, columns * CAP // 512, pack, 0)


def shear(slot_plane, shear_offsets, raw):
    columns = raw.shape[1]
    return pl.pallas_call(
        shear_kernel,
        out_shape=[
            jax.ShapeDtypeStruct((columns // 2, 16, 128), BF),
            jax.ShapeDtypeStruct((1, 128), I32),
        ],
        in_specs=[SM, SM, V],
        out_specs=[V, V],
        scratch_shapes=[
            pltpu.VMEM((2, SHEAR + columns, 128), F32),
            pltpu.VMEM((columns * CAP, 128), F32),
        ],
        compiler_params=params(24),
        name="shear",
    )(slot_plane, shear_offsets, raw)


def greet_all(g, q):
    barrier = pltpu.get_barrier_semaphore()

    def hello(k, carry):
        pl.semaphore_signal(barrier, inc=1, device_id=(lax.rem(g + k, NB), q), device_id_type=MESH)
        return carry

    lax.fori_loop(1, NB, hello, 0)
    pl.semaphore_wait(barrier, NB - 1)


def scatter_kernel(blocks, label_row, received, labels, send, recv, send_small, recv_small, own):
    g = lax.axis_index("gz")
    q = lax.axis_index("gy")
    greet_all(g, q)

    def pair(k, target):
        block = snake(target)
        big = pltpu.make_async_remote_copy(
            src_ref=blocks.at[pl.ds(block * 16, 16)],
            dst_ref=received.at[g],
            send_sem=send.at[k],
            recv_sem=recv.at[k],
            device_id=(target, q),
            device_id_type=MESH,
        )
        small = pltpu.make_async_remote_copy(
            src_ref=label_row,
            dst_ref=labels.at[g],
            send_sem=send_small.at[k],
            recv_sem=recv_small.at[k],
            device_id=(target, q),
            device_id_type=MESH,
        )
        return big, small

    def start(k, carry):
        for copy in pair(k, lax.rem(g + k, NB)):
            copy.start()
        return carry

    lax.fori_loop(1, NB, start, 0)
    mine = (
        pltpu.make_async_copy(blocks.at[pl.ds(snake(g) * 16, 16)], received.at[g], own.at[0]),
        pltpu.make_async_copy(label_row, labels.at[g], own.at[1]),
    )
    for copy in mine:
        copy.start()
    for copy in mine:
        copy.wait()

    def finish(k, carry):
        for copy in pair(k, lax.rem(g + k, NB)):
            copy.wait()
        return carry

    lax.fori_loop(1, NB, finish, 0)


def scatter(blocks, label_row):
    return pl.pallas_call(
        scatter_kernel,
        out_shape=[
            jax.ShapeDtypeStruct((NB, 16, 16, 128), BF),
            jax.ShapeDtypeStruct((NB, 1, 128), I32),
        ],
        in_specs=[ANY, ANY],
        out_specs=[ANY, ANY],
        scratch_shapes=[pltpu.SemaphoreType.DMA((NB,))] * 4 + [pltpu.SemaphoreType.DMA((2,))],
        compiler_params=params(8, collective_id=0, has_side_effects=True),
        name="scatter",
    )(blocks, label_row)


def collect_kernel(coded, peak, out, peaks, send, recv, send_small, recv_small, own):
    g = lax.axis_index("gz")
    q = lax.axis_index("gy")
    block = snake(g)
    greet_all(g, q)
    rows = pl.ds(pl.multiple_of(block * XB, XB), XB)

    def pair(k, target):
        big = pltpu.make_async_remote_copy(
            src_ref=coded.at[pl.ds(target * 4, 4)],
            dst_ref=out.at[:, rows, :],
            send_sem=send.at[k],
            recv_sem=recv.at[k],
            device_id=(target, q),
            device_id_type=MESH,
        )
        small = pltpu.make_async_remote_copy(
            src_ref=peak,
            dst_ref=peaks.at[block],
            send_sem=send_small.at[k],
            recv_sem=recv_small.at[k],
            device_id=(target, q),
            device_id_type=MESH,
        )
        return big, small

    def start(k, carry):
        for copy in pair(k, lax.rem(g + k, NB)):
            copy.start()
        return carry

    lax.fori_loop(1, NB, start, 0)
    mine = (
        pltpu.make_async_copy(coded.at[pl.ds(g * 4, 4)], out.at[:, rows, :], own.at[0]),
        pltpu.make_async_copy(peak, peaks.at[block], own.at[1]),
    )
    for copy in mine:
        copy.start()
    for copy in mine:
        copy.wait()

    def finish(k, carry):
        for copy in pair(k, lax.rem(g + k, NB)):
            copy.wait()
        return carry

    lax.fori_loop(1, NB, finish, 0)


def collect(coded, peak):
    return pl.pallas_call(
        collect_kernel,
        out_shape=[
            jax.ShapeDtypeStruct((4, NB * XB, 128), BF),
            jax.ShapeDtypeStruct((NB, 1, 128), F32),
        ],
        in_specs=[ANY, ANY],
        out_specs=[ANY, ANY],
        scratch_shapes=[pltpu.SemaphoreType.DMA((NB,))] * 4 + [pltpu.SemaphoreType.DMA((2,))],
        compiler_params=params(8, collective_id=1, has_side_effects=True),
        name="collect",
    )(coded, peak)


def halo_kernel(faces, packs, x_halo, y_halo, send, recv):
    g = lax.axis_index("gz")
    q = lax.axis_index("gy")
    b = snake(g)
    count = lax.axis_size("gy")
    up, down = snake(lax.rem(b + 1, NB)), snake(lax.rem(b + NB - 1, NB))
    right, left = lax.rem(q + 1, count), lax.rem(q + count - 1, count)
    barrier = pltpu.get_barrier_semaphore()
    around = [(d, e) for d in (down, g, up) for e in (left, q, right)]
    del around[4]
    for device in around:
        pl.semaphore_signal(barrier, inc=1, device_id=device, device_id_type=MESH)
    pl.semaphore_wait(barrier, 8)
    moves = [
        (faces.at[1, pl.ds(1, 7)], x_halo.at[0, pl.ds(1, 7)], (up, q)),
        (faces.at[0, pl.ds(0, 7)], x_halo.at[1, pl.ds(0, 7)], (down, q)),
        (packs.at[1], y_halo.at[0, pl.ds(1, 4)], (g, right)),
        (packs.at[0], y_halo.at[1, pl.ds(1, 4)], (g, left)),
        (packs.at[1, 3], y_halo.at[0, 0], (up, right)),
        (packs.at[1, 0], y_halo.at[0, 5], (down, right)),
        (packs.at[0, 3], y_halo.at[1, 0], (up, left)),
        (packs.at[0, 0], y_halo.at[1, 5], (down, left)),
    ]
    copies = [
        pltpu.make_async_remote_copy(
            src_ref=src, dst_ref=dst, send_sem=send.at[i], recv_sem=recv.at[i], device_id=device, device_id_type=MESH
        )
        for i, (src, dst, device) in enumerate(moves)
    ]
    for copy in copies:
        copy.start()
    for copy in copies:
        copy.wait()


def exchange(faces, packs, collective_id):
    return pl.pallas_call(
        halo_kernel,
        out_shape=[
            jax.ShapeDtypeStruct((2, 8, 128, 128), BF),
            jax.ShapeDtypeStruct((2, 6, 128, 128), BF),
        ],
        in_specs=[ANY, ANY],
        out_specs=[ANY, ANY],
        scratch_shapes=[pltpu.SemaphoreType.DMA((8,))] * 2,
        compiler_params=params(8, collective_id=collective_id, has_side_effects=True),
        name="halo",
    )(faces, packs)


def store_edges(group, values, edges, faces, packs):
    total = dot(values[0], edges[0])
    for s in range(1, 8):
        total += dot(values[s], edges[s])
    packs[0, group] = total[:, 0:128].astype(BF)
    packs[1, group] = total[:, 128:256].astype(BF)

    @pl.when(group == 0)
    def _():
        for s in range(8):
            faces[0, s] = values[s]

    @pl.when(group == 3)
    def _():
        for s in range(8):
            faces[1, s] = values[s]


def place_kernel(received, labels, edges, observed, faces, packs):
    lane = iota((128, 128), 1)
    plane = iota((128, 128), 0)
    parts = []
    for chunk in range(4):
        row = jnp.zeros((1, 128), I32)
        for j in range(8):
            row = jnp.where(lax.div(iota((1, 128), 1), 16) == j, labels[chunk * 8 + j], row)
        parts.append(row == plane)
    parity = lax.rem(lax.div(lane, CAP), 2)
    onehot = jnp.concatenate(
        [
            jnp.concatenate([jnp.where(hit & (parity == p), 1.0, 0.0).astype(BF) for hit in parts], axis=1)
            for p in range(2)
        ],
        axis=0,
    )

    def group(k, carry):
        values = []
        for j in range(4):
            both = dot(onehot, received[:, k * 4 + j].reshape(NB * 16, 128)).astype(BF)
            values += [both[0:128], both[128:256]]
        for s in range(8):
            observed[k * 8 + s] = values[s]
        store_edges(k, values, edges, faces, packs)
        return carry

    lax.fori_loop(0, 4, group, 0)


def place(received, labels, edges):
    return pl.pallas_call(
        place_kernel,
        out_shape=[
            jax.ShapeDtypeStruct((XB, 128, 128), BF),
            jax.ShapeDtypeStruct((2, 8, 128, 128), BF),
            jax.ShapeDtypeStruct((2, 4, 128, 128), BF),
        ],
        in_specs=[V] * 3,
        out_specs=[V] * 3,
        compiler_params=params(24),
        name="place",
    )(received, labels, edges)


def blur_block(main, x_halo, y_halo, px, wy_hi, wy_lo, bz_hl, mirror, dark_col, by_y, x_hi, x_lo, finish):
    b = snake(lax.axis_index("gz"))
    q = lax.axis_index("gy")
    inside = (b > 0, b < NB - 1)
    lane = lax.rem(iota((128, 128), 1), 16)
    outside_y = ((lane < 8) & (q == 0)) | ((lane >= 8) & (q == lax.axis_size("gy") - 1))

    def rows_halo(group):
        both = y_halo[0, group].astype(F32) + y_halo[1, group].astype(F32)
        if dark_col is not None:
            both += dark_col[...]
        return jnp.where(outside_y, 0.0, both)

    def along_y(at, s, v, halo):
        hi, lo = split(v)
        h_hi, h_lo = halo
        wide = jnp.concatenate([hi, h_hi], axis=1)
        total = dot(wide, wy_hi[0, s]) + dot(wide, wy_lo[0, s])
        if h_lo is None:
            total += dot(lo, wy_hi[0, s, 0:128])
        else:
            total += dot(jnp.concatenate([lo, h_lo], axis=1), wy_hi[0, s])
        by_y[at, 0:128] = total[:, 0:128]
        by_y[at, 128:256] = total[:, 128:256]

    def spread(halo):
        if dark_col is not None:
            return split(halo)
        return halo.astype(BF), None

    for side, group, members in ((0, 0, range(1, 8)), (1, 5, range(0, 7))):
        halo = spread(jnp.where(inside[side], rows_halo(group), 0.0))
        for s in members:
            v = x_halo[side, s].astype(F32)
            if dark_col is not None:
                v += dark_col[...]
            along_y(group * 8 + s, s, jnp.where(inside[side], v, 0.0), halo)

    def main_group(k, carry):
        halo = spread(rows_halo(k + 1))
        for s in range(8):
            along_y((k + 1) * 8 + s, s, main(k * 8 + s), halo)
        return carry

    lax.fori_loop(0, 4, main_group, 0)

    def along_x(t, carry):
        for r in range(2):
            rows = pl.ds(pl.multiple_of(r * 128 + t * 16, 16), 16)
            taps = [px[r, TX - 1 - j if mirror else j] for j in range(TX)]
            lines = [by_y[i, rows, :] for i in range(1, 47)]
            for x in range(XB):
                total = taps[0] * lines[x]
                for j in range(1, TX):
                    total += taps[j] * lines[x + j]
                hi, lo = split(total)
                x_hi[x, rows, :] = hi
                x_lo[x, rows, :] = lo
        return carry

    lax.fori_loop(0, 8, along_x, 0)

    def along_z(k, carry):
        results = []
        for j in range(0, 8, 2):
            x = k * 8 + j
            hi = jnp.concatenate([x_hi[x], x_hi[x + 1]], axis=1)
            lo = jnp.concatenate([x_lo[x], x_lo[x + 1]], axis=1)
            both = dot(bz_hl[0], hi)
            total = both[0:128] + both[128:256] + dot(bz_hl[0, 0:128], lo)
            results += [total[:, 0:128], total[:, 128:256]]
        finish(k, results)
        return carry

    lax.fori_loop(0, 4, along_z, 0)


SCRATCH = [
    pltpu.VMEM((48, 256, 128), F32),
    pltpu.VMEM((XB, 256, 128), BF),
    pltpu.VMEM((XB, 256, 128), BF),
]


def ratio_kernel(first, px, estimate, observed, x_halo, y_halo, dark_col, wy_hi, wy_lo, bz_hl, edges, quotient, faces, packs, *scratch):
    def main(x):
        if first:
            return estimate[x].astype(F32) + dark_col[...]
        return estimate[x]

    def finish(k, results):
        values = []
        for s in range(8):
            value = observed[k * 8 + s].astype(F32) / (results[s] + dark_col[...])
            quotient[k * 8 + s] = value
            values.append(value.astype(BF))
        store_edges(k, values, edges, faces, packs)

    blur_block(main, x_halo, y_halo, px, wy_hi, wy_lo, bz_hl, True, dark_col if first else None, *scratch, finish)


def kind_spec(shape, kind):
    return pl.BlockSpec((1,) + shape, lambda i: (kind,) + (0,) * len(shape))


def whole(*shape):
    return pl.BlockSpec(shape, lambda i: (0,) * len(shape))


def table_specs(kind):
    return [kind_spec((8, 256, 256), kind), kind_spec((8, 256, 256), kind), kind_spec((256, 256), kind)]


VOLUME = (XB, 128, 128)
FACES = (2, 8, 128, 128)
PACKS = (2, 4, 128, 128)
HALOS = [whole(*FACES), whole(2, 6, 128, 128)]


def ratio(first, estimate, observed, halos, tables, px):
    wy_hi, wy_lo, bz_hl, edges, dark_col = tables
    return pl.pallas_call(
        lambda *refs: ratio_kernel(first, *refs),
        grid=(1,),
        out_shape=[
            jax.ShapeDtypeStruct(VOLUME, F32),
            jax.ShapeDtypeStruct(FACES, BF),
            jax.ShapeDtypeStruct(PACKS, BF),
        ],
        in_specs=[SM, whole(*VOLUME), whole(*VOLUME), *HALOS, whole(128, 128), *table_specs(0), whole(8, 128, 256)],
        out_specs=[whole(*VOLUME), whole(*FACES), whole(*PACKS)],
        scratch_shapes=SCRATCH,
        compiler_params=params(44),
        name="ratio",
    )(px, estimate, observed, *halos, dark_col, wy_hi, wy_lo, bz_hl, edges)


def update_kernel(first, last, px, quotient, estimate, x_halo, y_halo, dark_col, wy_hi, wy_lo, bz_hl, edges, *refs):
    if last:
        coded, peak, woven, top, *scratch = refs
        top[...] = jnp.zeros_like(top)
    else:
        new, faces, packs, *scratch = refs

    def finish(k, results):
        values = []
        for s in range(8):
            x = k * 8 + s
            old = estimate[x]
            if first:
                old = old.astype(F32) + dark_col[...]
            value = old * results[s]
            if last:
                woven[pl.ds(x, 128, stride=XB), :] = value
                top[...] = jnp.maximum(top[...], value)
            else:
                new[x] = value
                values.append(value.astype(BF))
        if not last:
            store_edges(k, values, edges, faces, packs)

    blur_block(lambda x: quotient[x], x_halo, y_halo, px, wy_hi, wy_lo, bz_hl, False, None, *scratch, finish)
    if last:
        highest = jnp.max(top[...])
        scale = 2.0**15 / jnp.where(highest > 0.0, highest, 1.0)
        peak[...] = jnp.full((1, 128), highest, F32)

        def encode(i, carry):
            part = woven[pl.ds(pl.multiple_of(i * 256, 256), 256), :] * scale
            part = part * part
            part = part * part
            coded[pl.ds(i * 8, 8)] = (part * part).astype(BF).reshape(8, XB, 128)
            return carry

        lax.fori_loop(0, NZ // 8, encode, 0)


def update(first, last, quotient, estimate, halos, tables, px):
    wy_hi, wy_lo, bz_hl, edges, dark_col = tables
    if last:
        out_shape = [jax.ShapeDtypeStruct((NZ, XB, 128), BF), jax.ShapeDtypeStruct((1, 128), F32)]
        out_specs = [whole(NZ, XB, 128), whole(1, 128)]
        extra = [pltpu.VMEM((NZ * XB, 128), F32), pltpu.VMEM((128, 128), F32)]
    else:
        out_shape = [
            jax.ShapeDtypeStruct(VOLUME, F32),
            jax.ShapeDtypeStruct(FACES, BF),
            jax.ShapeDtypeStruct(PACKS, BF),
        ]
        out_specs = [whole(*VOLUME), whole(*FACES), whole(*PACKS)]
        extra = []
    return pl.pallas_call(
        lambda *refs: update_kernel(first, last, *refs),
        grid=(1,),
        out_shape=out_shape,
        in_specs=[SM, whole(*VOLUME), whole(*VOLUME), *HALOS, whole(128, 128), *table_specs(1), whole(8, 128, 256)],
        out_specs=out_specs,
        scratch_shapes=extra + SCRATCH,
        compiler_params=params(48),
        name="update",
    )(px, quotient, estimate, *halos, dark_col, wy_hi, wy_lo, bz_hl, edges)


def shards(raw_planes, slot_plane, shear_offsets, dark_level, profile_z, profile_x, profile_y):
    tables = make_tables(profile_z, profile_x, profile_y, dark_level)
    blocks, label_row = shear(slot_plane, shear_offsets, raw_planes)
    received, labels = scatter(blocks, label_row)
    observed, faces, packs = place(received, labels, tables[3])
    estimate = observed
    for iteration in range(ITERS):
        first, last = iteration == 0, iteration == ITERS - 1
        halos = exchange(faces, packs, 2)
        quotient, faces, packs = ratio(first, estimate, observed, halos, tables, profile_x)
        halos = exchange(faces, packs, 2)
        estimate, *rest = update(first, last, quotient, estimate, halos, tables, profile_x)
        if not last:
            faces, packs = rest
    coded, peaks = collect(estimate, rest[0])
    decoded = jnp.sqrt(jnp.sqrt(jnp.sqrt(coded.astype(F32)))).reshape(4, NB, XB, 128) * (peaks[None] * 2.0**-15)
    return decoded.reshape(4, NB * XB, 128)


def solution(mesh):
    in_specs = (P("gz", None, "gy"), P("gz"), P(), P(), P(), P(), P())
    out_specs = P("gz", None, "gy")
    return jax.shard_map(shards, mesh=mesh, in_specs=in_specs, out_specs=out_specs, check_vma=False)
```

```python
import jax
import jax.numpy as jnp
from jax import lax
from jax.experimental import pallas as pl
from jax.experimental.pallas import tpu as pltpu
from jax.sharding import PartitionSpec as P

SHEAR = 256
ITERS = 2
NZ = 128
NB = 32
XB = 32
YB = 128
CAP = 8
TX = 15
TZ = 41
MESH = pl.DeviceIdType.MESH
BF = jnp.bfloat16
F32 = jnp.float32
I32 = jnp.int32
V = pl.BlockSpec(memory_space=pltpu.VMEM)
SM = pl.BlockSpec(memory_space=pltpu.SMEM)
ANY = pl.BlockSpec(memory_space=pl.ANY)


def params(mib, **kw):
    return pltpu.CompilerParams(vmem_limit_bytes=mib * 2**20, **kw)


def snake(g):
    high = lax.div(g, 8)
    y = lax.rem(lax.div(g, 2), 4)
    flip = lax.rem(high, 2)
    return high * 8 + (y + flip * (3 - 2 * y)) * 2 + lax.rem(g, 2)


def iota(shape, dim):
    return lax.broadcasted_iota(I32, shape, dim)


def dot(a, b):
    return jnp.dot(a, b, preferred_element_type=F32)


def split(v):
    hi = v.astype(BF)
    return hi, (v - hi.astype(F32)).astype(BF)


def toeplitz(profile, r, distance, extent, mirror):
    total = jnp.zeros(distance.shape, F32)
    for d in range(extent):
        total = jnp.where(distance == d, profile[r, extent - 1 - d if mirror else d], total)
    return total


def tables_kernel(pz, px, py, dark, wy_hi, wy_lo, bz_hl, edges, dark_col):
    for kind in range(2):
        mirror = kind == 0
        for r in range(2):
            lanes = pl.ds(r * 128, 128)
            row = iota((128, 128), 0)
            col = iota((128, 128), 1)
            hi, lo = split(toeplitz(py, r, row - col + 7, TX, mirror))
            for s in range(8):
                wy_hi[kind, s, 0:128, lanes] = hi
                wy_lo[kind, s, 0:128, lanes] = lo
            h = lax.rem(row, 16)
            source = jnp.where(h < 8, h - 7, h + 120)
            distance = jnp.where(lax.rem(h, 8) == 7, -1, source - col + 7)
            halo = toeplitz(py, r, distance, TX, mirror)
            for s in range(8):
                hi, lo = split(jnp.where(lax.div(row, 16) == s, halo, 0.0))
                wy_hi[kind, s, 128:256, lanes] = hi
                wy_lo[kind, s, 128:256, lanes] = lo
            hi, lo = split(toeplitz(pz, r, col - row + TZ // 2, TZ, mirror))
            bz_hl[kind, 0:128, lanes] = hi
            bz_hl[kind, 128:256, lanes] = lo
    row = iota((128, 128), 0)
    col = iota((128, 128), 1)
    for s in range(8):
        near = (col == s * 16 + 8 + row) & (row < 7)
        far = (col == s * 16 + row - 121) & (row >= 121)
        edges[s, :, 0:128] = jnp.where(near, 1.0, 0.0).astype(BF)
        edges[s, :, 128:256] = jnp.where(far, 1.0, 0.0).astype(BF)
    level = jnp.sum(jnp.where(row == col, dark[...], 0.0), axis=1, keepdims=True)
    dark_col[...] = jnp.broadcast_to(level, (128, 128))


def make_tables(profile_z, profile_x, profile_y, dark_level):
    return pl.pallas_call(
        tables_kernel,
        out_shape=[
            jax.ShapeDtypeStruct((2, 8, 256, 256), BF),
            jax.ShapeDtypeStruct((2, 8, 256, 256), BF),
            jax.ShapeDtypeStruct((2, 256, 256), BF),
            jax.ShapeDtypeStruct((8, 128, 256), BF),
            jax.ShapeDtypeStruct((128, 128), F32),
        ],
        in_specs=[SM, SM, SM, V],
        out_specs=[V] * 5,
        compiler_params=params(24),
        name="tables",
    )(profile_z, profile_x, profile_y, dark_level.reshape(1, 128))


def shear_kernel(slot, offsets, raw, blocks, label_row, padded, woven):
    columns = raw.shape[1]
    lane = lax.rem(iota((1, 128), 1), CAP)
    labels = jnp.zeros((1, 128), I32)
    for k in range(2):
        padded[k, 0:SHEAR] = jnp.zeros((SHEAR, 128), F32)
    for c in range(CAP):
        plane = slot[c]
        labels = jnp.where(lane == c, plane, labels)
        start = SHEAR - offsets[jnp.maximum(plane, 0)]
        k = c % 2
        for x in range(0, columns, 256):
            padded[k, SHEAR + x : SHEAR + x + 256] = raw[c, x : x + 256].astype(F32)
        for x in range(0, columns, 256):
            woven[pl.ds(x * CAP + c, 256, stride=CAP), :] = padded[k, pl.ds(start + x, 256), :]
    label_row[...] = labels

    def pack(i, carry):
        at = pl.ds(pl.multiple_of(i * 512, 512), 512)
        blocks[pl.ds(i * 32, 32)] = woven[at, :].reshape(32, 16, 128).astype(BF)
        return carry

    lax.fori_loop(0, columns * CAP // 512, pack, 0)


def shear(slot_plane, shear_offsets, raw):
    columns = raw.shape[1]
    return pl.pallas_call(
        shear_kernel,
        out_shape=[
            jax.ShapeDtypeStruct((columns // 2, 16, 128), BF),
            jax.ShapeDtypeStruct((1, 128), I32),
        ],
        in_specs=[SM, SM, V],
        out_specs=[V, V],
        scratch_shapes=[
            pltpu.VMEM((2, SHEAR + columns, 128), F32),
            pltpu.VMEM((columns * CAP, 128), F32),
        ],
        compiler_params=params(24),
        name="shear",
    )(slot_plane, shear_offsets, raw)


def greet_all(g, q):
    barrier = pltpu.get_barrier_semaphore()

    def hello(k, carry):
        pl.semaphore_signal(barrier, inc=1, device_id=(lax.rem(g + k, NB), q), device_id_type=MESH)
        return carry

    lax.fori_loop(1, NB, hello, 0)
    pl.semaphore_wait(barrier, NB - 1)


def scatter_kernel(blocks, label_row, received, labels, send, recv, send_small, recv_small, own):
    g = lax.axis_index("gz")
    q = lax.axis_index("gy")
    greet_all(g, q)

    def pair(k, target):
        block = snake(target)
        big = pltpu.make_async_remote_copy(
            src_ref=blocks.at[pl.ds(block * 16, 16)],
            dst_ref=received.at[g],
            send_sem=send.at[k],
            recv_sem=recv.at[k],
            device_id=(target, q),
            device_id_type=MESH,
        )
        small = pltpu.make_async_remote_copy(
            src_ref=label_row,
            dst_ref=labels.at[g],
            send_sem=send_small.at[k],
            recv_sem=recv_small.at[k],
            device_id=(target, q),
            device_id_type=MESH,
        )
        return big, small

    def start(k, carry):
        for copy in pair(k, lax.rem(g + k, NB)):
            copy.start()
        return carry

    lax.fori_loop(1, NB, start, 0)
    mine = (
        pltpu.make_async_copy(blocks.at[pl.ds(snake(g) * 16, 16)], received.at[g], own.at[0]),
        pltpu.make_async_copy(label_row, labels.at[g], own.at[1]),
    )
    for copy in mine:
        copy.start()
    for copy in mine:
        copy.wait()

    def finish(k, carry):
        for copy in pair(k, lax.rem(g + k, NB)):
            copy.wait()
        return carry

    lax.fori_loop(1, NB, finish, 0)


def scatter(blocks, label_row):
    return pl.pallas_call(
        scatter_kernel,
        out_shape=[
            jax.ShapeDtypeStruct((NB, 16, 16, 128), BF),
            jax.ShapeDtypeStruct((NB, 1, 128), I32),
        ],
        in_specs=[ANY, ANY],
        out_specs=[ANY, ANY],
        scratch_shapes=[pltpu.SemaphoreType.DMA((NB,))] * 4 + [pltpu.SemaphoreType.DMA((2,))],
        compiler_params=params(8, collective_id=0, has_side_effects=True),
        name="scatter",
    )(blocks, label_row)


def onehot_of(labels):
    plane = iota((128, 128), 0)
    lane = iota((128, 128), 1)
    spot = lax.div(iota((1, 128), 1), 16)
    parts = []
    for chunk in range(4):
        row = jnp.zeros((1, 128), I32)
        for j in range(8):
            row = jnp.where(spot == j, labels[chunk * 8 + j], row)
        parts.append(row == plane)
    parity = lax.rem(lax.div(lane, CAP), 2)
    return jnp.concatenate(
        [
            jnp.concatenate([jnp.where(hit & (parity == p), 1.0, 0.0).astype(BF) for hit in parts], axis=1)
            for p in range(2)
        ],
        axis=0,
    )


STEPS = 2 * ITERS
MOVES = 14


def solve_kernel(
    px, received, labels, dark_col, wy_hi, wy_lo, bz_hl, edges, out, peaks,
    observed, estimate, by_y, x_hi, x_lo, faces, packs, x_halo, y_halo, coded, peak, woven, top,
    send, recv, send_big, recv_big, send_small, recv_small, own,
):
    g = lax.axis_index("gz")
    q = lax.axis_index("gy")
    b = snake(g)
    count = lax.axis_size("gy")
    up, down = snake(lax.rem(b + 1, NB)), snake(lax.rem(b + NB - 1, NB))
    right, left = lax.rem(q + 1, count), lax.rem(q + count - 1, count)

    barrier = pltpu.get_barrier_semaphore()

    def hello(k, carry):
        pl.semaphore_signal(barrier, inc=1, device_id=(lax.rem(g + k, NB), q), device_id_type=MESH)
        return carry

    lax.fori_loop(1, NB, hello, 0)
    for device in [(d, e) for d in (down, g, up) for e in (left, right)]:
        pl.semaphore_signal(barrier, inc=1, device_id=device, device_id_type=MESH)
    pl.semaphore_wait(barrier, NB - 1 + 6)

    def move(i, n, src, dst, device):
        return pltpu.make_async_remote_copy(
            src_ref=src,
            dst_ref=dst,
            send_sem=send.at[i, n],
            recv_sem=recv.at[i, n],
            device_id=device,
            device_id_type=MESH,
        )

    def pack_moves(i, k):
        return [
            move(i, k, packs.at[i, 1, k], y_halo.at[i, 0, k + 1], (g, right)),
            move(i, 4 + k, packs.at[i, 0, k], y_halo.at[i, 1, k + 1], (g, left)),
        ]

    def face_down(i):
        return move(i, 8, faces.at[i, 0, pl.ds(0, 7)], x_halo.at[i, 1, pl.ds(0, 7)], (down, q))

    def face_up(i):
        return move(i, 9, faces.at[i, 1, pl.ds(1, 7)], x_halo.at[i, 0, pl.ds(1, 7)], (up, q))

    def first_corners(i):
        return [
            move(i, 10, packs.at[i, 1, 0], y_halo.at[i, 0, 5], (down, right)),
            move(i, 11, packs.at[i, 0, 0], y_halo.at[i, 1, 5], (down, left)),
        ]

    def last_corners(i):
        return [
            move(i, 12, packs.at[i, 1, 3], y_halo.at[i, 0, 0], (up, right)),
            move(i, 13, packs.at[i, 0, 3], y_halo.at[i, 1, 0], (up, left)),
        ]

    def all_moves(i):
        return [m for k in range(4) for m in pack_moves(i, k)] + [face_down(i), face_up(i)] + first_corners(i) + last_corners(i)

    def emit(i, k, values):
        @pl.when(k == 0)
        def _():
            for s in range(8):
                faces[i, 0, s] = values[s]
            face_down(i).start()

        @pl.when(k == 3)
        def _():
            for s in range(8):
                faces[i, 1, s] = values[s]
            face_up(i).start()

        total = dot(jnp.concatenate(values, axis=1), edges[...].reshape(1024, 256))
        packs[i, 0, k] = total[:, 0:128].astype(BF)
        packs[i, 1, k] = total[:, 128:256].astype(BF)

        @pl.when(k == 0)
        def _():
            for m in first_corners(i):
                m.start()

        @pl.when(k == 3)
        def _():
            for m in last_corners(i):
                m.start()

        for m in pack_moves(i, k):
            m.start()

    def along_y(at, values, kind):
        pairs = [split(v) for v in values]
        hi = jnp.concatenate([p[0] for p in pairs], axis=0)
        lo = jnp.concatenate([p[1] for p in pairs], axis=0)
        upper = wy_hi[kind, 0, 0:128]
        total = dot(jnp.concatenate([hi, lo], axis=1), jnp.concatenate([upper, upper], axis=0))
        total += dot(hi, wy_lo[kind, 0, 0:128])
        for s in range(len(values)):
            by_y[at + s, 0:128] = total[s * 128 : s * 128 + 128, 0:128]
            by_y[at + s, 128:256] = total[s * 128 : s * 128 + 128, 128:256]

    lane = lax.rem(iota((128, 128), 1), 16)
    outside_y = ((lane < 8) & (q == 0)) | ((lane >= 8) & (q == count - 1))

    def add_halo(i, group, members, kind, keep):
        halo = y_halo[i, 0, group].astype(F32) + y_halo[i, 1, group].astype(F32)
        if i == 0:
            halo += dark_col[...]
        halo = jnp.where(outside_y, 0.0, halo)
        if keep is not None:
            halo = jnp.where(keep, halo, 0.0)
        hi, lo = split(halo)
        both = jnp.concatenate([hi, lo], axis=1)
        for s in members:
            upper = wy_hi[kind, s, 128:256]
            if i == 0:
                total = dot(both, jnp.concatenate([upper, upper], axis=0))
            else:
                total = dot(hi, upper)
            total += dot(hi, wy_lo[kind, s, 128:256])
            at = group * 8 + s
            by_y[at, 0:128] += total[:, 0:128]
            by_y[at, 128:256] += total[:, 128:256]

    def along_x(mirror, spans):
        def tile(t, carry):
            for r in range(2):
                rows = pl.ds(pl.multiple_of(r * 128 + t * 16, 16), 16)
                for x, n in spans:
                    total = jnp.zeros((n, 16, 128), F32)
                    for j in range(TX):
                        total += px[r, TX - 1 - j if mirror else j] * by_y[x + 1 + j : x + 1 + j + n, rows, :]
                    hi, lo = split(total)
                    x_hi[x : x + n, rows, :] = hi
                    x_lo[x : x + n, rows, :] = lo
            return carry

        lax.fori_loop(0, 8, tile, 0)

    def along_z(k, kind):
        results = []
        for j in range(0, 8, 2):
            x = k * 8 + j
            hi = jnp.concatenate([x_hi[x], x_hi[x + 1]], axis=1)
            lo = jnp.concatenate([x_lo[x], x_lo[x + 1]], axis=1)
            both = dot(bz_hl[kind], hi)
            total = both[0:128] + both[128:256] + dot(bz_hl[kind, 0:128], lo)
            results += [total[:, 0:128], total[:, 128:256]]
        return results

    def in_order(j):
        return jnp.where(j == 0, 0, jnp.where(j == 1, 3, j - 1))

    onehot = onehot_of(labels)

    def start_group(j, carry):
        k = in_order(j)
        values = []
        for p in range(4):
            both = dot(onehot, received[:, k * 4 + p].reshape(NB * 16, 128))
            values += [both[0:128], both[128:256]]
        for s in range(8):
            observed[k * 8 + s] = values[s].astype(BF)
        emit(0, k, [v.astype(BF) for v in values])
        values = [v + dark_col[...] for v in values]
        for s in range(8):
            estimate[k * 8 + s] = values[s]
        along_y(8 + k * 8, values, 0)
        return carry

    lax.fori_loop(0, 4, start_group, 0)
    top[...] = jnp.zeros_like(top)

    for i in range(STEPS):
        kind = i % 2
        last = i == STEPS - 1
        moves = all_moves(i)
        for m in moves[0:8]:
            m.wait_recv()

        def main_halo(k, carry, i=i, kind=kind):
            add_halo(i, k + 1, range(8), kind, None)
            return carry

        lax.fori_loop(0, 4, main_halo, 0)
        along_x(kind == 0, [(7, 9), (16, 9)])
        for m in moves[8:]:
            m.wait_recv()
        for side, group, members, keep in ((0, 0, range(1, 8), b > 0), (1, 5, range(0, 7), b < NB - 1)):
            values = []
            for s in members:
                v = x_halo[i, side, s].astype(F32)
                if i == 0:
                    v += dark_col[...]
                values.append(jnp.where(keep, v, 0.0))
            along_y(group * 8 + members[0], values, kind)
            add_halo(i, group, members, kind, keep)
        along_x(kind == 0, [(0, 7), (25, 7)])

        def end_group(j, carry, i=i, kind=kind, last=last):
            k = in_order(j)
            results = along_z(k, kind)
            values = []
            for s in range(8):
                x = k * 8 + s
                if kind == 0:
                    value = observed[x].astype(F32) / (results[s] + dark_col[...])
                else:
                    value = estimate[x] * results[s]
                    if last:
                        woven[pl.ds(x, 128, stride=XB), :] = value
                        top[...] = jnp.maximum(top[...], value)
                    else:
                        estimate[x] = value
                values.append(value)
            if not last:
                emit(i + 1, k, [v.astype(BF) for v in values])
                along_y(8 + k * 8, values, 1 - kind)
            return carry

        lax.fori_loop(0, 4, end_group, 0)

    highest = jnp.max(top[...])
    scale = 2.0**15 / jnp.where(highest > 0.0, highest, 1.0)
    peak[...] = jnp.full((1, 128), highest, F32)

    def encode(n, carry):
        part = woven[pl.ds(pl.multiple_of(n * 256, 256), 256), :] * scale
        part = part * part
        part = part * part
        coded[pl.ds(n * 8, 8)] = (part * part).astype(BF).reshape(8, XB, 128)
        return carry

    lax.fori_loop(0, NZ // 8, encode, 0)
    rows = pl.ds(pl.multiple_of(b * XB, XB), XB)

    def pair(k, target):
        big = pltpu.make_async_remote_copy(
            src_ref=coded.at[pl.ds(target * 4, 4)],
            dst_ref=out.at[:, rows, :],
            send_sem=send_big.at[k],
            recv_sem=recv_big.at[k],
            device_id=(target, q),
            device_id_type=MESH,
        )
        small = pltpu.make_async_remote_copy(
            src_ref=peak,
            dst_ref=peaks.at[b],
            send_sem=send_small.at[k],
            recv_sem=recv_small.at[k],
            device_id=(target, q),
            device_id_type=MESH,
        )
        return big, small

    def start(k, carry):
        for copy in pair(k, lax.rem(g + k, NB)):
            copy.start()
        return carry

    lax.fori_loop(1, NB, start, 0)
    mine = (
        pltpu.make_async_copy(coded.at[pl.ds(g * 4, 4)], out.at[:, rows, :], own.at[0]),
        pltpu.make_async_copy(peak, peaks.at[b], own.at[1]),
    )
    for copy in mine:
        copy.start()
    for i in range(STEPS):
        for m in all_moves(i):
            m.wait_send()
    for copy in mine:
        copy.wait()

    def finish(k, carry):
        for copy in pair(k, lax.rem(g + k, NB)):
            copy.wait()
        return carry

    lax.fori_loop(1, NB, finish, 0)


def solve(received, labels, tables, px):
    wy_hi, wy_lo, bz_hl, edges, dark_col = tables
    dma = pltpu.SemaphoreType.DMA
    return pl.pallas_call(
        solve_kernel,
        out_shape=[
            jax.ShapeDtypeStruct((4, NB * XB, 128), BF),
            jax.ShapeDtypeStruct((NB, 1, 128), F32),
        ],
        in_specs=[SM] + [V] * 7,
        out_specs=[ANY, ANY],
        scratch_shapes=[
            pltpu.VMEM((XB, 128, 128), BF),
            pltpu.VMEM((XB, 128, 128), F32),
            pltpu.VMEM((48, 256, 128), F32),
            pltpu.VMEM((XB, 256, 128), BF),
            pltpu.VMEM((XB, 256, 128), BF),
            pltpu.VMEM((STEPS, 2, 8, 128, 128), BF),
            pltpu.VMEM((STEPS, 2, 4, 128, 128), BF),
            pltpu.VMEM((STEPS, 2, 8, 128, 128), BF),
            pltpu.VMEM((STEPS, 2, 6, 128, 128), BF),
            pltpu.VMEM((NZ, XB, 128), BF),
            pltpu.VMEM((1, 128), F32),
            pltpu.VMEM((NZ * XB, 128), F32),
            pltpu.VMEM((128, 128), F32),
            dma((STEPS, MOVES)),
            dma((STEPS, MOVES)),
            dma((NB,)),
            dma((NB,)),
            dma((NB,)),
            dma((NB,)),
            dma((2,)),
        ],
        compiler_params=params(44, collective_id=1, has_side_effects=True),
        name="solve",
    )(px, received, labels, dark_col, wy_hi, wy_lo, bz_hl, edges)


def shards(raw_planes, slot_plane, shear_offsets, dark_level, profile_z, profile_x, profile_y):
    tables = make_tables(profile_z, profile_x, profile_y, dark_level)
    blocks, label_row = shear(slot_plane, shear_offsets, raw_planes)
    received, labels = scatter(blocks, label_row)
    coded, peaks = solve(received, labels, tables, profile_x)
    decoded = jnp.sqrt(jnp.sqrt(jnp.sqrt(coded.astype(F32)))).reshape(4, NB, XB, 128) * (peaks[None] * 2.0**-15)
    return decoded.reshape(4, NB * XB, 128)


def solution(mesh):
    in_specs = (P("gz", None, "gy"), P("gz"), P(), P(), P(), P(), P())
    out_specs = P("gz", None, "gy")
    return jax.shard_map(shards, mesh=mesh, in_specs=in_specs, out_specs=out_specs, check_vma=False)
```

```python
import jax
import jax.numpy as jnp
from jax import lax
from jax.experimental import pallas as pl
from jax.experimental.pallas import tpu as pltpu
from jax.sharding import PartitionSpec as P

SHEAR = 256
ITERS = 2
NZ = 128
NB = 32
XB = 32
YB = 128
CAP = 8
TX = 15
TZ = 41
MESH = pl.DeviceIdType.MESH
BF = jnp.bfloat16
F32 = jnp.float32
I32 = jnp.int32
V = pl.BlockSpec(memory_space=pltpu.VMEM)
SM = pl.BlockSpec(memory_space=pltpu.SMEM)
ANY = pl.BlockSpec(memory_space=pl.ANY)


def params(mib, **kw):
    return pltpu.CompilerParams(vmem_limit_bytes=mib * 2**20, **kw)


def snake(g):
    high = lax.div(g, 8)
    y = lax.rem(lax.div(g, 2), 4)
    flip = lax.rem(high, 2)
    return high * 8 + (y + flip * (3 - 2 * y)) * 2 + lax.rem(g, 2)


def iota(shape, dim):
    return lax.broadcasted_iota(I32, shape, dim)


def dot(a, b):
    return jnp.dot(a, b, preferred_element_type=F32)


def split(v):
    hi = v.astype(BF)
    return hi, (v - hi.astype(F32)).astype(BF)


def toeplitz(profile, r, distance, extent, mirror):
    total = jnp.zeros(distance.shape, F32)
    for d in range(extent):
        total = jnp.where(distance == d, profile[r, extent - 1 - d if mirror else d], total)
    return total


def fill_tables(pz, py, dark, wy, wh, spread, bz_hl, dark_col, dark_pack):
    row = iota((128, 128), 0)
    col = iota((128, 128), 1)
    level = jnp.sum(jnp.where(row == col, dark[...], 0.0), axis=1, keepdims=True)
    dark_col[...] = jnp.broadcast_to(level, (128, 128))
    tile = jnp.zeros((16, 128), F32)
    for n in range(8):
        tile = jnp.where(lax.div(iota((16, 128), 1), 16) == n, dark_col[n * 16 : n * 16 + 16], tile)
    for n in range(8):
        dark_pack[n * 16 : n * 16 + 16] = tile
        lane = lax.rem(n * 16 + col, 128)
        spread[n] = jnp.where((row == lane) & ((col < 7) | (col >= 121)), 1.0, 0.0).astype(BF)
    for kind in range(2):
        mirror = kind == 0
        for r in range(2):
            lanes = pl.ds(r * 128, 128)
            hi, lo = split(toeplitz(py, r, row - col + 7, TX, mirror))
            wy[kind, 0:128, lanes] = hi
            wy[kind, 128:256, lanes] = hi
            wy[kind, 256:384, lanes] = lo
            h = lax.rem(row, 16)
            delta = lax.rem(col - (row - h) + 192, 128) - 64
            distance = h - 1 - delta
            near = (h > 0) & (h < 8) & (delta >= 0) & (delta < 7)
            far = (h > 7) & (h < 15) & (delta < 0) & (delta > -8)
            hi, lo = split(toeplitz(py, r, jnp.where(near | far, distance, -1), TX, mirror))
            wh[kind, 0:128, lanes] = hi
            wh[kind, 128:256, lanes] = lo
            hi, lo = split(toeplitz(pz, r, col - row + TZ // 2, TZ, mirror))
            bz_hl[kind, 0:128, lanes] = hi
            bz_hl[kind, 128:256, lanes] = lo


def onehot_of(labels):
    plane = iota((128, 128), 0)
    lane = iota((128, 128), 1)
    spot = lax.div(iota((1, 128), 1), 16)
    parts = []
    for chunk in range(4):
        row = jnp.zeros((1, 128), I32)
        for j in range(8):
            row = jnp.where(spot == j, labels[chunk * 8 + j], row)
        parts.append(row == plane)
    parity = lax.rem(lax.div(lane, CAP), 2)
    return jnp.concatenate(
        [
            jnp.concatenate([jnp.where(hit & (parity == p), 1.0, 0.0).astype(BF) for hit in parts], axis=1)
            for p in range(2)
        ],
        axis=0,
    )


STEPS = 2 * ITERS
MOVES = 14
WIDE = XB + TX - 1
ROWS = 256


def whole_kernel(
    slot, offsets, pz, px, py, raw_hbm, dark, out, peaks,
    raw, padded, woven, blocks, label_row, received, labels, wy, wh, spread, bz_hl, dark_col, dark_pack,
    observed, estimate, e_hi, e_lo, by_a, by_b, by_x, y_rim, x_rim, x_hi, x_lo, faces, packs, x_halo, y_halo, coded, peak, final, top,
    load, send_raw, recv_raw, send_label, recv_label, send, recv, send_big, recv_big, send_small, recv_small, own,
):
    g = lax.axis_index("gz")
    q = lax.axis_index("gy")
    b = snake(g)
    count = lax.axis_size("gy")
    up, down = snake(lax.rem(b + 1, NB)), snake(lax.rem(b + NB - 1, NB))
    right, left = lax.rem(q + 1, count), lax.rem(q + count - 1, count)

    for c in range(CAP):
        pltpu.make_async_copy(raw_hbm.at[c], raw.at[c], load.at[c]).start()
    barrier = pltpu.get_barrier_semaphore()

    def hello(k, carry):
        pl.semaphore_signal(barrier, inc=1, device_id=(lax.rem(g + k, NB), q), device_id_type=MESH)
        return carry

    lax.fori_loop(1, NB, hello, 0)
    for device in [(d, e) for d in (down, g, up) for e in (left, right)]:
        pl.semaphore_signal(barrier, inc=1, device_id=device, device_id_type=MESH)


    label_lane = lax.rem(iota((1, 128), 1), CAP)
    row = jnp.zeros((1, 128), I32)
    for c in range(CAP):
        row = jnp.where(label_lane == c, slot[c], row)
    label_row[...] = row
    for c in range(CAP):
        padded[c, 0:SHEAR] = jnp.zeros((SHEAR, 128), F32)
    for c in range(CAP):
        pltpu.make_async_copy(raw_hbm.at[c], raw.at[c], load.at[c]).wait()

        def widen(n, carry, c=c):
            padded[c, pl.ds(pl.multiple_of(SHEAR + n * ROWS, ROWS), ROWS)] = raw[
                c, pl.ds(pl.multiple_of(n * ROWS, ROWS), ROWS)
            ].astype(F32)
            return carry

        lax.fori_loop(0, NB * XB // ROWS, widen, 0)
    pl.semaphore_wait(barrier, NB - 1 + 6)

    def block_to(target):
        return pltpu.make_async_remote_copy(
            src_ref=blocks.at[pl.ds(snake(target) * 16, 16)],
            dst_ref=received.at[g],
            send_sem=send_raw.at[target],
            recv_sem=recv_raw.at[g],
            device_id=(target, q),
            device_id_type=MESH,
        )

    def label_to(target):
        return pltpu.make_async_remote_copy(
            src_ref=label_row,
            dst_ref=labels.at[g],
            send_sem=send_label.at[target],
            recv_sem=recv_label.at[g],
            device_id=(target, q),
            device_id_type=MESH,
        )

    def block_from(source):
        return pltpu.make_async_remote_copy(
            src_ref=blocks.at[pl.ds(0, 16)],
            dst_ref=received.at[source],
            send_sem=send_raw.at[source],
            recv_sem=recv_raw.at[source],
            device_id=(source, q),
            device_id_type=MESH,
        )

    def label_from(source):
        return pltpu.make_async_remote_copy(
            src_ref=label_row,
            dst_ref=labels.at[source],
            send_sem=send_label.at[source],
            recv_sem=recv_label.at[source],
            device_id=(source, q),
            device_id_type=MESH,
        )

    def turn(n):
        return jnp.where(n == 0, 1, jnp.where(n == 1, 3, jnp.where(n == 2, 2, 0)))

    def shear_rows(n, carry):
        part = lax.rem(lax.div(g, 8) + turn(n), 4)
        x = part * ROWS
        for c in range(CAP):
            start = SHEAR - offsets[jnp.maximum(slot[c], 0)] + x
            woven[pl.ds(c, ROWS, stride=CAP), :] = padded[c, pl.ds(start, ROWS), :]
        for m in range(0, ROWS // 2, 32):
            at = pl.ds(pl.multiple_of(part * (ROWS // 2) + m, 32), 32)
            blocks[at] = woven[m * 16 : m * 16 + 512, :].reshape(32, 16, 128).astype(BF)

        def start_one(m, carry):
            target = snake(part * 8 + m)

            @pl.when(target != g)
            def _():
                block_to(target).start()
                label_to(target).start()

            return carry

        lax.fori_loop(0, 8, start_one, 0)
        return carry

    lax.fori_loop(0, NB * XB // ROWS, shear_rows, 0)
    mine = (
        pltpu.make_async_copy(blocks.at[pl.ds(b * 16, 16)], received.at[g], own.at[0]),
        pltpu.make_async_copy(label_row, labels.at[g], own.at[1]),
    )
    for copy in mine:
        copy.start()
    fill_tables(pz, py, dark, wy, wh, spread, bz_hl, dark_col, dark_pack)
    top[...] = jnp.zeros_like(top)
    for copy in mine:
        copy.wait()

    def arrive(k, carry):
        source = lax.rem(g + k, NB)
        block_from(source).wait_recv()
        label_from(source).wait_recv()
        return carry

    lax.fori_loop(1, NB, arrive, 0)


    def move(i, n, src, dst, device):
        return pltpu.make_async_remote_copy(
            src_ref=src,
            dst_ref=dst,
            send_sem=send.at[i, n],
            recv_sem=recv.at[i, n],
            device_id=device,
            device_id_type=MESH,
        )

    def pack_moves(i, k):
        return [
            move(i, k, packs.at[i, k], y_halo.at[i, 0, k + 1], (g, right)),
            move(i, 4 + k, packs.at[i, k], y_halo.at[i, 1, k + 1], (g, left)),
        ]

    def face_down(i):
        return move(i, 8, faces.at[i, 0, pl.ds(0, 7)], x_halo.at[i, 1, pl.ds(0, 7)], (down, q))

    def face_up(i):
        return move(i, 9, faces.at[i, 1, pl.ds(1, 7)], x_halo.at[i, 0, pl.ds(1, 7)], (up, q))

    def first_corners(i):
        return [
            move(i, 10, packs.at[i, 0, pl.ds(0, 112)], y_halo.at[i, 0, 5, pl.ds(0, 112)], (down, right)),
            move(i, 11, packs.at[i, 0, pl.ds(0, 112)], y_halo.at[i, 1, 5, pl.ds(0, 112)], (down, left)),
        ]

    def last_corners(i):
        return [
            move(i, 12, packs.at[i, 3, pl.ds(16, 112)], y_halo.at[i, 0, 0, pl.ds(16, 112)], (up, right)),
            move(i, 13, packs.at[i, 3, pl.ds(16, 112)], y_halo.at[i, 1, 0, pl.ds(16, 112)], (up, left)),
        ]

    def all_moves(i):
        moves = [m for k in range(4) for m in pack_moves(i, k)]
        return moves + [face_down(i), face_up(i)] + first_corners(i) + last_corners(i)

    chunk_of_lane = lax.div(iota((16, 128), 1), 16)

    def emit(i, k, values):
        @pl.when(k == 0)
        def _():
            for s in range(8):
                faces[i, 0, s] = values[s].astype(BF)
            face_down(i).start()

        @pl.when(k == 3)
        def _():
            for s in range(8):
                faces[i, 1, s] = values[s].astype(BF)
            face_up(i).start()

        for c in range(8):
            tile = jnp.zeros((16, 128), F32)
            for n in range(8):
                turned = pltpu.roll(values[c][n * 16 : n * 16 + 16], (n * 16 + 8) % 128, 1)
                tile = jnp.where(chunk_of_lane == n, turned, tile)
            packs[i, k, c * 16 : c * 16 + 16] = tile.astype(BF)
        for m in pack_moves(i, k):
            m.start()

    def emit_corners(i):
        for m in first_corners(i) + last_corners(i):
            m.start()

    lane = iota((128, 128), 1)
    lane16 = lax.rem(lane, 16)
    outside_y = ((lane16 < 8) & (q == 0)) | ((lane16 >= 8) & (q == count - 1))

    def rim_y(i, group, kind, keep):
        halo = jnp.where(lane16 < 8, y_halo[i, 0, group].astype(F32), y_halo[i, 1, group].astype(F32))
        if i == 0:
            halo += dark_pack[...]
        halo = jnp.where(outside_y, 0.0, halo)
        if keep is not None:
            halo = jnp.where(keep, halo, 0.0)
        halo = halo.astype(BF)
        total = dot(jnp.concatenate([halo, halo], axis=1), wh[kind])
        for r in range(2):
            y_rim[r, pl.ds(group * 8, 8)] = total[:, r * 128 : r * 128 + 128].reshape(8, 16, 128)

    def rim_x(mirror):
        for r in range(2):
            for x in range(0, XB, 8):
                total = px[r, TX - 1 if mirror else 0] * y_rim[r, x + 1 : x + 9]
                for j in range(1, TX):
                    total += px[r, TX - 1 - j if mirror else j] * y_rim[r, x + 1 + j : x + 9 + j]
                hi, lo = split(total)
                x_rim[r, x : x + 8, :, 0:128] = hi
                x_rim[r, x : x + 8, :, 128:256] = lo

    def add_rim(n, carry):
        place = jnp.concatenate([spread[2 * n], spread[2 * n + 1]], axis=1)
        for r in range(2):
            rim = x_rim[r].reshape(XB * 16, 256)
            added = dot(rim, jnp.concatenate([place, place], axis=0))
            for half in range(2):
                rows = pl.ds(pl.multiple_of(r * 128 + n * 32 + half * 16, 16), 16)
                part = added[:, half * 128 : half * 128 + 128].reshape(XB, 16, 128)
                hi, lo = split(by_x[:, rows, :] + part)
                x_hi[:, rows, :] = hi
                x_lo[:, rows, :] = lo
        return carry


    def y_piece(t, h, into, kind, first, n):
        rows = pl.ds(pl.multiple_of(t * 16, 16), 16)
        at = pl.ds(pl.multiple_of(h * 16, 16), 16)
        hi, lo = (e[first : first + n, rows, :].reshape(n * 16, 128) for e in (e_hi, e_lo))
        total = dot(jnp.concatenate([hi, lo, hi], axis=1), wy[kind])
        for r in range(2):
            into[r, first : first + n, at] = total[:, r * 128 : r * 128 + 128].reshape(n, 16, 128)

    def x_piece(t, h, source, mirror, first, n):
        at = pl.ds(pl.multiple_of(h * 16, 16), 16)
        for r in range(2):
            total = px[r, TX - 1 if mirror else 0] * source[r, first : first + n, at]
            for j in range(1, TX):
                total += px[r, TX - 1 - j if mirror else j] * source[r, first + j : first + j + n, at]
            rows = pl.ds(pl.multiple_of(r * 128 + t * 16, 16), 16)
            by_x[first : first + n, rows, :] = total

    def along_yx(kind, y_spans, x_spans):
        mirror = kind == 0
        for span in y_spans:
            y_piece(0, 0, by_a, kind, *span)

        def two(n, carry):
            for span in y_spans:
                y_piece(2 * n + 1, n, by_b, kind, *span)
            for span in x_spans:
                x_piece(2 * n, n, by_a, mirror, *span)
            later = jnp.minimum(n + 1, 3)
            for span in y_spans:
                y_piece(2 * later, later, by_a, kind, *span)
            for span in x_spans:
                x_piece(2 * n + 1, n, by_b, mirror, *span)
            return carry

        lax.fori_loop(0, 4, two, 0)

    def along_z(k, kind):
        results = []
        for j in range(0, 8, 2):
            x = k * 8 + j
            hi = jnp.concatenate([x_hi[x], x_hi[x + 1]], axis=1)
            lo = jnp.concatenate([x_lo[x], x_lo[x + 1]], axis=1)
            both = dot(bz_hl[kind], hi)
            total = both[0:128] + both[128:256] + dot(bz_hl[kind, 0:128], lo)
            results += [total[:, 0:128], total[:, 128:256]]
        return results

    def in_order(j):
        return jnp.where(j == 0, 0, jnp.where(j == 1, 3, j - 1))

    def keep_columns(k, values):
        pairs = [split(v) for v in values]
        for s in range(8):
            e_hi[7 + k * 8 + s] = pairs[s][0]
            e_lo[7 + k * 8 + s] = pairs[s][1]

    onehot = onehot_of(labels)

    def start_group(j, carry):
        k = in_order(j)
        values = []
        for p in range(4):
            both = dot(onehot, received[:, k * 4 + p].reshape(NB * 16, 128))
            values += [both[0:128], both[128:256]]
        for s in range(8):
            observed[k * 8 + s] = values[s].astype(BF)
        emit(0, k, values)
        values = [v + dark_col[...] for v in values]
        for s in range(8):
            estimate[k * 8 + s] = values[s]
        keep_columns(k, values)
        return carry

    lax.fori_loop(0, 4, start_group, 0)
    emit_corners(0)

    for i in range(STEPS):
        kind = i % 2
        last = i == STEPS - 1
        moves = all_moves(i)
        along_yx(kind, [(7, 32)], [(7, 5), (12, 4), (16, 5), (21, 4)])
        for m in moves[0:8]:
            m.wait_recv()

        def main_rim(k, carry, i=i, kind=kind):
            rim_y(i, k + 1, kind, None)
            return carry

        lax.fori_loop(0, 4, main_rim, 0)
        for m in moves[8:10]:
            m.wait_recv()
        for side, members, at, keep in ((0, range(1, 8), 0, b > 0), (1, range(0, 7), 39, b < NB - 1)):
            for n, s in enumerate(members):
                v = x_halo[i, side, s].astype(F32)
                if i == 0:
                    v += dark_col[...]
                v = jnp.where(keep, v, 0.0)
                if i == 0:
                    e_hi[at + n], e_lo[at + n] = split(v)
                else:
                    e_hi[at + n] = v.astype(BF)
                    e_lo[at + n] = jnp.zeros((128, 128), BF)
        along_yx(kind, [(0, 7), (39, 7)], [(0, 4), (4, 3), (25, 4), (29, 3)])
        for m in moves[10:]:
            m.wait_recv()
        rim_y(i, 0, kind, b > 0)
        rim_y(i, 5, kind, b < NB - 1)
        rim_x(kind == 0)
        lax.fori_loop(0, 4, add_rim, 0)

        def end_group(j, carry, i=i, kind=kind, last=last):
            k = in_order(j)
            results = along_z(k, kind)
            values = []
            for s in range(8):
                x = k * 8 + s
                if kind == 0:
                    value = observed[x].astype(F32) / (results[s] + dark_col[...])
                else:
                    value = estimate[x] * results[s]
                    if last:
                        final[pl.ds(x, 128, stride=XB), :] = value
                        top[...] = jnp.maximum(top[...], value)
                    else:
                        estimate[x] = value
                values.append(value)
            if not last:
                emit(i + 1, k, values)
                keep_columns(k, values)
            return carry

        lax.fori_loop(0, 4, end_group, 0)
        if not last:
            emit_corners(i + 1)


    highest = jnp.max(top[...])
    scale = 2.0**15 / jnp.where(highest > 0.0, highest, 1.0)
    peak[...] = jnp.full((1, 128), highest, F32)

    def encode(n, carry):
        part = final[pl.ds(pl.multiple_of(n * 256, 256), 256), :] * scale
        part = part * part
        part = part * part
        coded[pl.ds(n * 8, 8)] = (part * part).astype(BF).reshape(8, XB, 128)
        return carry

    lax.fori_loop(0, NZ // 8, encode, 0)
    rows = pl.ds(pl.multiple_of(b * XB, XB), XB)

    def pair(target):
        big = pltpu.make_async_remote_copy(
            src_ref=coded.at[pl.ds(target * 4, 4)],
            dst_ref=out.at[:, rows, :],
            send_sem=send_big.at[target],
            recv_sem=recv_big.at[g],
            device_id=(target, q),
            device_id_type=MESH,
        )
        small = pltpu.make_async_remote_copy(
            src_ref=peak,
            dst_ref=peaks.at[b],
            send_sem=send_small.at[target],
            recv_sem=recv_small.at[g],
            device_id=(target, q),
            device_id_type=MESH,
        )
        return big, small

    def pair_from(source):
        block = snake(source)
        big = pltpu.make_async_remote_copy(
            src_ref=coded.at[pl.ds(0, 4)],
            dst_ref=out.at[:, pl.ds(pl.multiple_of(block * XB, XB), XB), :],
            send_sem=send_big.at[source],
            recv_sem=recv_big.at[source],
            device_id=(source, q),
            device_id_type=MESH,
        )
        small = pltpu.make_async_remote_copy(
            src_ref=peak,
            dst_ref=peaks.at[block],
            send_sem=send_small.at[source],
            recv_sem=recv_small.at[source],
            device_id=(source, q),
            device_id_type=MESH,
        )
        return big, small

    def start(m, carry):
        for n in (1, 3, 2):
            for copy in pair(lax.rem(g + 8 * n, NB) // 8 * 8 + lax.rem(g + m, 8)):
                copy.start()
        return carry

    lax.fori_loop(0, 8, start, 0)

    def start_own(m, carry):
        for copy in pair(g // 8 * 8 + lax.rem(g + m, 8)):
            copy.start()
        return carry

    lax.fori_loop(1, 8, start_own, 0)
    mine = (
        pltpu.make_async_copy(coded.at[pl.ds(g * 4, 4)], out.at[:, rows, :], own.at[0]),
        pltpu.make_async_copy(peak, peaks.at[b], own.at[1]),
    )
    for copy in mine:
        copy.start()

    def sent(k, carry):
        target = lax.rem(g + k, NB)
        block_to(target).wait_send()
        label_to(target).wait_send()
        return carry

    lax.fori_loop(1, NB, sent, 0)
    for i in range(STEPS):
        for m in all_moves(i):
            m.wait_send()
    for copy in mine:
        copy.wait()

    def finish(k, carry):
        other = lax.rem(g + k, NB)
        for copy in pair(other):
            copy.wait_send()
        for copy in pair_from(other):
            copy.wait_recv()
        return carry

    lax.fori_loop(1, NB, finish, 0)


def decode_kernel(coded, peaks, out):
    for n in range(NB):
        at = pl.ds(n * XB, XB)
        root = lax.rsqrt(lax.rsqrt(jnp.maximum(coded[0, at].astype(F32), 2.0**-120)))
        out[0, at] = root * lax.rsqrt(root) * (peaks[n] * 2.0**-15)


def decode(coded, peaks):
    return pl.pallas_call(
        decode_kernel,
        grid=(coded.shape[0],),
        out_shape=jax.ShapeDtypeStruct(coded.shape, F32),
        in_specs=[
            pl.BlockSpec((1,) + coded.shape[1:], lambda i: (i, 0, 0)),
            pl.BlockSpec(peaks.shape, lambda i: (0, 0, 0)),
        ],
        out_specs=pl.BlockSpec((1,) + coded.shape[1:], lambda i: (i, 0, 0)),
        compiler_params=params(8),
        name="decode",
    )(coded, peaks)


def shards(raw_planes, slot_plane, shear_offsets, dark_level, profile_z, profile_x, profile_y):
    columns = raw_planes.shape[1]
    dma = pltpu.SemaphoreType.DMA
    vmem = pltpu.VMEM
    coded, peaks = pl.pallas_call(
        whole_kernel,
        out_shape=[
            jax.ShapeDtypeStruct((4, columns, 128), BF),
            jax.ShapeDtypeStruct((NB, 1, 128), F32),
        ],
        in_specs=[SM] * 5 + [ANY, V],
        out_specs=[ANY, ANY],
        scratch_shapes=[
            vmem((CAP, columns, 128), BF),
            vmem((CAP, SHEAR + columns, 128), F32),
            vmem((ROWS * CAP, 128), F32),
            vmem((columns // 2, 16, 128), BF),
            vmem((1, 128), I32),
            vmem((NB, 16, 16, 128), BF),
            vmem((NB, 1, 128), I32),
            vmem((2, 384, 256), BF),
            vmem((2, 256, 256), BF),
            vmem((8, 128, 128), BF),
            vmem((2, 256, 256), BF),
            vmem((128, 128), F32),
            vmem((128, 128), F32),
            vmem((XB, 128, 128), BF),
            vmem((XB, 128, 128), F32),
            vmem((WIDE, 128, 128), BF),
            vmem((WIDE, 128, 128), BF),
            vmem((2, WIDE, 64, 128), F32),
            vmem((2, WIDE, 64, 128), F32),
            vmem((XB, 256, 128), F32),
            vmem((2, 48, 16, 128), F32),
            vmem((2, XB, 16, 256), BF),
            vmem((XB, 256, 128), BF),
            vmem((XB, 256, 128), BF),
            vmem((STEPS, 2, 8, 128, 128), BF),
            vmem((STEPS, 4, 128, 128), BF),
            vmem((STEPS, 2, 8, 128, 128), BF),
            vmem((STEPS, 2, 6, 128, 128), BF),
            vmem((NZ, XB, 128), BF),
            vmem((1, 128), F32),
            vmem((NZ * XB, 128), F32),
            vmem((128, 128), F32),
            dma((CAP,)),
            dma((NB,)),
            dma((NB,)),
            dma((NB,)),
            dma((NB,)),
            dma((STEPS, MOVES)),
            dma((STEPS, MOVES)),
            dma((NB,)),
            dma((NB,)),
            dma((NB,)),
            dma((NB,)),
            dma((2,)),
        ],
        compiler_params=params(56, collective_id=0, has_side_effects=True),
        name="deconvolve",
    )(slot_plane, shear_offsets, profile_z, profile_x, profile_y, raw_planes, dark_level.reshape(1, 128))
    return decode(coded, peaks)


def solution(mesh):
    in_specs = (P("gz", None, "gy"), P("gz"), P(), P(), P(), P(), P())
    out_specs = P("gz", None, "gy")
    return jax.shard_map(shards, mesh=mesh, in_specs=in_specs, out_specs=out_specs, check_vma=False)
```

```python
import jax
import jax.numpy as jnp
from jax import lax
from jax.experimental import pallas as pl
from jax.experimental.pallas import tpu as pltpu
from jax.sharding import PartitionSpec as P

SHEAR = 256
ITERS = 2
NZ = 128
NB = 32
XB = 32
YB = 128
CAP = 8
TX = 15
TZ = 41
MESH = pl.DeviceIdType.MESH
BF = jnp.bfloat16
F32 = jnp.float32
I32 = jnp.int32
V = pl.BlockSpec(memory_space=pltpu.VMEM)
SM = pl.BlockSpec(memory_space=pltpu.SMEM)
ANY = pl.BlockSpec(memory_space=pl.ANY)


def params(mib, **kw):
    return pltpu.CompilerParams(vmem_limit_bytes=mib * 2**20, **kw)


def snake(g):
    high = lax.div(g, 8)
    y = lax.rem(lax.div(g, 2), 4)
    flip = lax.rem(high, 2)
    return high * 8 + (y + flip * (3 - 2 * y)) * 2 + lax.rem(g, 2)


def iota(shape, dim):
    return lax.broadcasted_iota(I32, shape, dim)


def dot(a, b):
    return jnp.dot(a, b, preferred_element_type=F32)


def split(v):
    hi = v.astype(BF)
    return hi, (v - hi.astype(F32)).astype(BF)


def toeplitz(profile, r, distance, extent, mirror):
    total = jnp.zeros(distance.shape, F32)
    for d in range(extent):
        total = jnp.where(distance == d, profile[r, extent - 1 - d if mirror else d], total)
    return total


def fill_tables(pz, py, dark, wy, wh, spread, bz_hl, dark_col, dark_pack):
    row = iota((128, 128), 0)
    col = iota((128, 128), 1)
    level = jnp.sum(jnp.where(row == col, dark[...], 0.0), axis=1, keepdims=True)
    dark_col[...] = jnp.broadcast_to(level, (128, 128))
    tile = jnp.zeros((16, 128), F32)
    for n in range(8):
        tile = jnp.where(lax.div(iota((16, 128), 1), 16) == n, dark_col[n * 16 : n * 16 + 16], tile)
    for n in range(8):
        dark_pack[n * 16 : n * 16 + 16] = tile
        lane = lax.rem(n * 16 + col, 128)
        spread[n] = jnp.where((row == lane) & ((col < 7) | (col >= 121)), 1.0, 0.0).astype(BF)
    for kind in range(2):
        mirror = kind == 0
        for r in range(2):
            lanes = pl.ds(r * 128, 128)
            hi, lo = split(toeplitz(py, r, row - col + 7, TX, mirror))
            wy[kind, 0:128, lanes] = hi
            wy[kind, 128:256, lanes] = hi
            wy[kind, 256:384, lanes] = lo
            h = lax.rem(row, 16)
            delta = lax.rem(col - (row - h) + 192, 128) - 64
            distance = h - 1 - delta
            near = (h > 0) & (h < 8) & (delta >= 0) & (delta < 7)
            far = (h > 7) & (h < 15) & (delta < 0) & (delta > -8)
            hi, lo = split(toeplitz(py, r, jnp.where(near | far, distance, -1), TX, mirror))
            wh[kind, 0:128, lanes] = hi
            wh[kind, 128:256, lanes] = lo
            hi, lo = split(toeplitz(pz, r, col - row + TZ // 2, TZ, mirror))
            bz_hl[kind, 0:128, lanes] = hi
            bz_hl[kind, 128:256, lanes] = lo


def onehot_of(labels):
    plane = iota((128, 128), 0)
    lane = iota((128, 128), 1)
    spot = lax.div(iota((1, 128), 1), 16)
    parts = []
    for chunk in range(4):
        row = jnp.zeros((1, 128), I32)
        for j in range(8):
            row = jnp.where(spot == j, labels[chunk * 8 + j], row)
        parts.append(row == plane)
    parity = lax.rem(lax.div(lane, CAP), 2)
    return jnp.concatenate(
        [
            jnp.concatenate([jnp.where(hit & (parity == p), 1.0, 0.0).astype(BF) for hit in parts], axis=1)
            for p in range(2)
        ],
        axis=0,
    )


STEPS = 2 * ITERS
MOVES = 14
WIDE = XB + TX - 1
ROWS = 256


def whole_kernel(
    slot, offsets, pz, px, py, raw_hbm, dark, out, peaks,
    raw, padded, woven, blocks, label_row, received, labels, wy, wh, spread, bz_hl, dark_col, dark_pack,
    observed, estimate, e_hi, e_lo, by_a, by_b, by_x, y_rim, x_rim, x_hi, x_lo, faces, packs, x_halo, y_halo, coded, peak, final, top,
    load, send_raw, recv_raw, send_label, recv_label, send, recv, send_big, recv_big, send_small, recv_small, own,
):
    g = lax.axis_index("gz")
    q = lax.axis_index("gy")
    b = snake(g)
    count = lax.axis_size("gy")
    up, down = snake(lax.rem(b + 1, NB)), snake(lax.rem(b + NB - 1, NB))
    right, left = lax.rem(q + 1, count), lax.rem(q + count - 1, count)

    for c in range(CAP):
        pltpu.make_async_copy(raw_hbm.at[c], raw.at[c], load.at[c]).start()
    barrier = pltpu.get_barrier_semaphore()

    def hello(k, carry):
        pl.semaphore_signal(barrier, inc=1, device_id=(lax.rem(g + k, NB), q), device_id_type=MESH)
        return carry

    lax.fori_loop(1, NB, hello, 0)
    for device in [(d, e) for d in (down, g, up) for e in (left, right)]:
        pl.semaphore_signal(barrier, inc=1, device_id=device, device_id_type=MESH)


    label_lane = lax.rem(iota((1, 128), 1), CAP)
    row = jnp.zeros((1, 128), I32)
    for c in range(CAP):
        row = jnp.where(label_lane == c, slot[c], row)
    label_row[...] = row
    for c in range(CAP):
        padded[c, 0:SHEAR] = jnp.zeros((SHEAR, 128), F32)
    for c in range(CAP):
        pltpu.make_async_copy(raw_hbm.at[c], raw.at[c], load.at[c]).wait()

        def widen(n, carry, c=c):
            padded[c, pl.ds(pl.multiple_of(SHEAR + n * ROWS, ROWS), ROWS)] = raw[
                c, pl.ds(pl.multiple_of(n * ROWS, ROWS), ROWS)
            ].astype(F32)
            return carry

        lax.fori_loop(0, NB * XB // ROWS, widen, 0)
    pl.semaphore_wait(barrier, NB - 1 + 6)

    def block_to(target):
        return pltpu.make_async_remote_copy(
            src_ref=blocks.at[pl.ds(snake(target) * 16, 16)],
            dst_ref=received.at[g],
            send_sem=send_raw.at[target],
            recv_sem=recv_raw.at[g],
            device_id=(target, q),
            device_id_type=MESH,
        )

    def label_to(target):
        return pltpu.make_async_remote_copy(
            src_ref=label_row,
            dst_ref=labels.at[g],
            send_sem=send_label.at[target],
            recv_sem=recv_label.at[g],
            device_id=(target, q),
            device_id_type=MESH,
        )

    def block_from(source):
        return pltpu.make_async_remote_copy(
            src_ref=blocks.at[pl.ds(0, 16)],
            dst_ref=received.at[source],
            send_sem=send_raw.at[source],
            recv_sem=recv_raw.at[source],
            device_id=(source, q),
            device_id_type=MESH,
        )

    def label_from(source):
        return pltpu.make_async_remote_copy(
            src_ref=label_row,
            dst_ref=labels.at[source],
            send_sem=send_label.at[source],
            recv_sem=recv_label.at[source],
            device_id=(source, q),
            device_id_type=MESH,
        )

    def turn(n):
        return jnp.where(n == 0, 1, jnp.where(n == 1, 3, jnp.where(n == 2, 2, 0)))

    def shear_rows(n, carry):
        part = lax.rem(lax.div(g, 8) + turn(n), 4)
        x = part * ROWS
        for c in range(CAP):
            start = SHEAR - offsets[jnp.maximum(slot[c], 0)] + x
            woven[pl.ds(c, ROWS, stride=CAP), :] = padded[c, pl.ds(start, ROWS), :]
        for m in range(0, ROWS // 2, 32):
            at = pl.ds(pl.multiple_of(part * (ROWS // 2) + m, 32), 32)
            blocks[at] = woven[m * 16 : m * 16 + 512, :].reshape(32, 16, 128).astype(BF)

        def start_one(m, carry):
            target = snake(part * 8 + m)

            @pl.when(target != g)
            def _():
                block_to(target).start()
                label_to(target).start()

            return carry

        lax.fori_loop(0, 8, start_one, 0)
        return carry

    lax.fori_loop(0, NB * XB // ROWS, shear_rows, 0)
    mine = (
        pltpu.make_async_copy(blocks.at[pl.ds(b * 16, 16)], received.at[g], own.at[0]),
        pltpu.make_async_copy(label_row, labels.at[g], own.at[1]),
    )
    for copy in mine:
        copy.start()
    fill_tables(pz, py, dark, wy, wh, spread, bz_hl, dark_col, dark_pack)
    top[...] = jnp.zeros_like(top)
    for copy in mine:
        copy.wait()

    def arrive(k, carry):
        source = lax.rem(g + k, NB)
        block_from(source).wait_recv()
        label_from(source).wait_recv()
        return carry

    lax.fori_loop(1, NB, arrive, 0)


    def move(i, n, src, dst, device):
        return pltpu.make_async_remote_copy(
            src_ref=src,
            dst_ref=dst,
            send_sem=send.at[i, n],
            recv_sem=recv.at[i, n],
            device_id=device,
            device_id_type=MESH,
        )

    def pack_moves(i, k):
        return [
            move(i, k, packs.at[i, k], y_halo.at[i, 0, k + 1], (g, right)),
            move(i, 4 + k, packs.at[i, k], y_halo.at[i, 1, k + 1], (g, left)),
        ]

    def face_down(i):
        return move(i, 8, faces.at[i, 0, pl.ds(0, 7)], x_halo.at[i, 1, pl.ds(0, 7)], (down, q))

    def face_up(i):
        return move(i, 9, faces.at[i, 1, pl.ds(1, 7)], x_halo.at[i, 0, pl.ds(1, 7)], (up, q))

    def first_corners(i):
        return [
            move(i, 10, packs.at[i, 0, pl.ds(0, 112)], y_halo.at[i, 0, 5, pl.ds(0, 112)], (down, right)),
            move(i, 11, packs.at[i, 0, pl.ds(0, 112)], y_halo.at[i, 1, 5, pl.ds(0, 112)], (down, left)),
        ]

    def last_corners(i):
        return [
            move(i, 12, packs.at[i, 3, pl.ds(16, 112)], y_halo.at[i, 0, 0, pl.ds(16, 112)], (up, right)),
            move(i, 13, packs.at[i, 3, pl.ds(16, 112)], y_halo.at[i, 1, 0, pl.ds(16, 112)], (up, left)),
        ]

    def all_moves(i):
        moves = [m for k in range(4) for m in pack_moves(i, k)]
        return moves + [face_down(i), face_up(i)] + first_corners(i) + last_corners(i)

    chunk_of_lane = lax.div(iota((16, 128), 1), 16)

    def pack(i, k, values):
        for c in range(8):
            tile = jnp.zeros((16, 128), F32)
            for n in range(8):
                turned = pltpu.roll(values[c][n * 16 : n * 16 + 16], (n * 16 + 8) % 128, 1)
                tile = jnp.where(chunk_of_lane == n, turned, tile)
            packs[i, k, c * 16 : c * 16 + 16] = tile.astype(BF)

    def emit(i, j):
        @pl.when(j == 0)
        def _():
            face_down(i).start()
            face_up(i).start()

        for k in (j, 3 - j):
            for m in pack_moves(i, k):
                m.start()

    def emit_corners(i):
        for m in first_corners(i) + last_corners(i):
            m.start()

    lane = iota((128, 128), 1)
    lane16 = lax.rem(lane, 16)
    outside_y = ((lane16 < 8) & (q == 0)) | ((lane16 >= 8) & (q == count - 1))

    def rim_y(i, group, n, kind, keep):
        outside = jnp.concatenate([outside_y] * n, axis=0)
        before = jnp.concatenate([lane16 < 8] * n, axis=0)
        sides = [y_halo[i, side, group : group + n].reshape(n * 128, 128).astype(F32) for side in range(2)]
        halo = jnp.where(before, sides[0], sides[1])
        if i == 0:
            halo += jnp.concatenate([dark_pack[...]] * n, axis=0)
        halo = jnp.where(outside, 0.0, halo)
        if keep is not None:
            halo = jnp.where(keep, halo, 0.0)
        halo = halo.astype(BF)
        total = dot(jnp.concatenate([halo, halo], axis=1), wh[kind])
        for r in range(2):
            y_rim[r, group * 8 : (group + n) * 8] = total[:, r * 128 : r * 128 + 128].reshape(n * 8, 16, 128)

    def rim_x(mirror):
        for r in range(2):
            for x in range(0, XB, 8):
                total = px[r, TX - 1 if mirror else 0] * y_rim[r, x + 1 : x + 9]
                for j in range(1, TX):
                    total += px[r, TX - 1 - j if mirror else j] * y_rim[r, x + 1 + j : x + 9 + j]
                hi, lo = split(total)
                x_rim[r, x : x + 8, :, 0:128] = hi
                x_rim[r, x : x + 8, :, 128:256] = lo

    def add_rim(n, carry):
        place = jnp.concatenate([spread[2 * n], spread[2 * n + 1]], axis=1)
        for r in range(2):
            rim = x_rim[r].reshape(XB * 16, 256)
            added = dot(rim, jnp.concatenate([place, place], axis=0))
            for half in range(2):
                rows = pl.ds(pl.multiple_of(r * 128 + n * 32 + half * 16, 16), 16)
                part = added[:, half * 128 : half * 128 + 128].reshape(XB, 16, 128)
                hi, lo = split(by_x[:, rows, :] + part)
                x_hi[:, rows, :] = hi
                x_lo[:, rows, :] = lo
        return carry


    def y_piece(t, h, into, kind, first, n):
        rows = pl.ds(pl.multiple_of(t * 16, 16), 16)
        at = pl.ds(pl.multiple_of(h * 16, 16), 16)
        hi, lo = (e[first : first + n, rows, :].reshape(n * 16, 128) for e in (e_hi, e_lo))
        total = dot(jnp.concatenate([hi, lo, hi], axis=1), wy[kind])
        for r in range(2):
            into[r, first : first + n, at] = total[:, r * 128 : r * 128 + 128].reshape(n, 16, 128)

    def x_piece(t, h, source, mirror, first, n):
        at = pl.ds(pl.multiple_of(h * 16, 16), 16)
        for r in range(2):
            total = px[r, TX - 1 if mirror else 0] * source[r, first : first + n, at]
            for j in range(1, TX):
                total += px[r, TX - 1 - j if mirror else j] * source[r, first + j : first + j + n, at]
            rows = pl.ds(pl.multiple_of(r * 128 + t * 16, 16), 16)
            by_x[first : first + n, rows, :] = total

    def along_yx(kind, y_spans, x_spans):
        mirror = kind == 0
        for span in y_spans:
            y_piece(0, 0, by_a, kind, *span)

        def two(n, carry):
            for span in y_spans:
                y_piece(2 * n + 1, n, by_b, kind, *span)
            for span in x_spans:
                x_piece(2 * n, n, by_a, mirror, *span)
            later = jnp.minimum(n + 1, 3)
            for span in y_spans:
                y_piece(2 * later, later, by_a, kind, *span)
            for span in x_spans:
                x_piece(2 * n + 1, n, by_b, mirror, *span)
            return carry

        lax.fori_loop(0, 4, two, 0)

    def along_z(k, kind):
        results = []
        for j in range(0, 8, 2):
            x = k * 8 + j
            hi = jnp.concatenate([x_hi[x], x_hi[x + 1]], axis=1)
            lo = jnp.concatenate([x_lo[x], x_lo[x + 1]], axis=1)
            both = dot(bz_hl[kind], hi)
            total = both[0:128] + both[128:256] + dot(bz_hl[kind, 0:128], lo)
            results += [total[:, 0:128], total[:, 128:256]]
        return results

    def keep_columns(k, values):
        pairs = [split(v) for v in values]
        for s in range(8):
            e_hi[7 + k * 8 + s] = pairs[s][0]
            e_lo[7 + k * 8 + s] = pairs[s][1]

    onehot = onehot_of(labels)

    def store_faces(i, j, first, second):
        @pl.when(j == 0)
        def _():
            for s in range(8):
                faces[i, 0, s] = first[s]
                faces[i, 1, s] = second[s]

    def start_groups(j, carry):
        for k in (j, 3 - j):
            values = []
            for p in range(4):
                both = dot(onehot, received[:, k * 4 + p].reshape(NB * 16, 128))
                values += [both[0:128], both[128:256]]
            for s in range(8):
                observed[k * 8 + s] = values[s].astype(BF)
            pack(0, k, values)
            values = [v + dark_col[...] for v in values]
            for s in range(8):
                estimate[k * 8 + s] = values[s]
            keep_columns(k, values)
        store_faces(0, j, [observed[s] for s in range(8)], [observed[XB - 8 + s] for s in range(8)])
        emit(0, j)
        return carry

    lax.fori_loop(0, 2, start_groups, 0)
    emit_corners(0)

    for i in range(STEPS):
        kind = i % 2
        last = i == STEPS - 1
        moves = all_moves(i)
        along_yx(kind, [(7, 32)], [(7, 5), (12, 4), (16, 5), (21, 4)])
        for m in moves[0:8]:
            m.wait_recv()

        rim_y(i, 1, 4, kind, None)
        for m in moves[8:10]:
            m.wait_recv()
        for side, members, at, keep in ((0, range(1, 8), 0, b > 0), (1, range(0, 7), 39, b < NB - 1)):
            for n, s in enumerate(members):
                v = x_halo[i, side, s].astype(F32)
                if i == 0:
                    v += dark_col[...]
                v = jnp.where(keep, v, 0.0)
                if i == 0:
                    e_hi[at + n], e_lo[at + n] = split(v)
                else:
                    e_hi[at + n] = v.astype(BF)
                    if i == 1:
                        e_lo[at + n] = jnp.zeros((128, 128), BF)
        along_yx(kind, [(0, 7), (39, 7)], [(0, 4), (4, 3), (25, 4), (29, 3)])
        for m in moves[10:]:
            m.wait_recv()
        rim_y(i, 0, 1, kind, b > 0)
        rim_y(i, 5, 1, kind, b < NB - 1)
        rim_x(kind == 0)
        lax.fori_loop(0, 4, add_rim, 0)

        def end_groups(j, carry, i=i, kind=kind, last=last):
            for k in (j, 3 - j):
                results = along_z(k, kind)
                values = []
                for s in range(8):
                    x = k * 8 + s
                    if kind == 0:
                        value = observed[x].astype(F32) / (results[s] + dark_col[...])
                    else:
                        value = estimate[x] * results[s]
                        if last:
                            final[pl.ds(x, 128, stride=XB), :] = value
                            top[...] = jnp.maximum(top[...], value)
                        else:
                            estimate[x] = value
                    values.append(value)
                if not last:
                    pack(i + 1, k, values)
                    keep_columns(k, values)
            if not last:
                store_faces(
                    i + 1, j, [e_hi[7 + s] for s in range(8)], [e_hi[7 + XB - 8 + s] for s in range(8)]
                )
                emit(i + 1, j)
            return carry

        lax.fori_loop(0, 2, end_groups, 0)
        if not last:
            emit_corners(i + 1)


    highest = jnp.max(top[...])
    scale = 2.0**15 / jnp.where(highest > 0.0, highest, 1.0)
    peak[...] = jnp.full((1, 128), highest, F32)

    def encode(n, carry):
        part = final[pl.ds(pl.multiple_of(n * 256, 256), 256), :] * scale
        part = part * part
        part = part * part
        coded[pl.ds(n * 8, 8)] = (part * part).astype(BF).reshape(8, XB, 128)
        return carry

    lax.fori_loop(0, NZ // 8, encode, 0)
    rows = pl.ds(pl.multiple_of(b * XB, XB), XB)

    def pair(target):
        big = pltpu.make_async_remote_copy(
            src_ref=coded.at[pl.ds(target * 4, 4)],
            dst_ref=out.at[:, rows, :],
            send_sem=send_big.at[target],
            recv_sem=recv_big.at[g],
            device_id=(target, q),
            device_id_type=MESH,
        )
        small = pltpu.make_async_remote_copy(
            src_ref=peak,
            dst_ref=peaks.at[b],
            send_sem=send_small.at[target],
            recv_sem=recv_small.at[g],
            device_id=(target, q),
            device_id_type=MESH,
        )
        return big, small

    def pair_from(source):
        block = snake(source)
        big = pltpu.make_async_remote_copy(
            src_ref=coded.at[pl.ds(0, 4)],
            dst_ref=out.at[:, pl.ds(pl.multiple_of(block * XB, XB), XB), :],
            send_sem=send_big.at[source],
            recv_sem=recv_big.at[source],
            device_id=(source, q),
            device_id_type=MESH,
        )
        small = pltpu.make_async_remote_copy(
            src_ref=peak,
            dst_ref=peaks.at[block],
            send_sem=send_small.at[source],
            recv_sem=recv_small.at[source],
            device_id=(source, q),
            device_id_type=MESH,
        )
        return big, small

    def start(m, carry):
        for n in (1, 3, 2):
            for copy in pair(lax.rem(g + 8 * n, NB) // 8 * 8 + lax.rem(g + m, 8)):
                copy.start()
        return carry

    lax.fori_loop(0, 8, start, 0)

    def start_own(m, carry):
        for copy in pair(g // 8 * 8 + lax.rem(g + m, 8)):
            copy.start()
        return carry

    lax.fori_loop(1, 8, start_own, 0)
    mine = (
        pltpu.make_async_copy(coded.at[pl.ds(g * 4, 4)], out.at[:, rows, :], own.at[0]),
        pltpu.make_async_copy(peak, peaks.at[b], own.at[1]),
    )
    for copy in mine:
        copy.start()

    def sent(k, carry):
        target = lax.rem(g + k, NB)
        block_to(target).wait_send()
        label_to(target).wait_send()
        return carry

    lax.fori_loop(1, NB, sent, 0)
    for i in range(STEPS):
        for m in all_moves(i):
            m.wait_send()
    for copy in mine:
        copy.wait()

    def finish(k, carry):
        other = lax.rem(g + k, NB)
        for copy in pair(other):
            copy.wait_send()
        for copy in pair_from(other):
            copy.wait_recv()
        return carry

    lax.fori_loop(1, NB, finish, 0)


def decode_kernel(coded, peaks, out):
    for n in range(NB):
        at = pl.ds(n * XB, XB)
        root = lax.rsqrt(lax.rsqrt(jnp.maximum(coded[:, at].astype(F32), 2.0**-120)))
        out[:, at] = root * lax.rsqrt(root) * (peaks[n] * 2.0**-15)


def decode(coded, peaks):
    return pl.pallas_call(
        decode_kernel,
        grid=(coded.shape[0] // 2,),
        out_shape=jax.ShapeDtypeStruct(coded.shape, F32),
        in_specs=[
            pl.BlockSpec((2,) + coded.shape[1:], lambda i: (i, 0, 0)),
            pl.BlockSpec(peaks.shape, lambda i: (0, 0, 0)),
        ],
        out_specs=pl.BlockSpec((2,) + coded.shape[1:], lambda i: (i, 0, 0)),
        compiler_params=params(60),
        name="decode",
    )(coded, peaks)


def shards(raw_planes, slot_plane, shear_offsets, dark_level, profile_z, profile_x, profile_y):
    columns = raw_planes.shape[1]
    dma = pltpu.SemaphoreType.DMA
    vmem = pltpu.VMEM
    coded, peaks = pl.pallas_call(
        whole_kernel,
        out_shape=[
            jax.ShapeDtypeStruct((4, columns, 128), BF),
            jax.ShapeDtypeStruct((NB, 1, 128), F32),
        ],
        in_specs=[SM] * 5 + [ANY, V],
        out_specs=[ANY, ANY],
        scratch_shapes=[
            vmem((CAP, columns, 128), BF),
            vmem((CAP, SHEAR + columns, 128), F32),
            vmem((ROWS * CAP, 128), F32),
            vmem((columns // 2, 16, 128), BF),
            vmem((1, 128), I32),
            vmem((NB, 16, 16, 128), BF),
            vmem((NB, 1, 128), I32),
            vmem((2, 384, 256), BF),
            vmem((2, 256, 256), BF),
            vmem((8, 128, 128), BF),
            vmem((2, 256, 256), BF),
            vmem((128, 128), F32),
            vmem((128, 128), F32),
            vmem((XB, 128, 128), BF),
            vmem((XB, 128, 128), F32),
            vmem((WIDE, 128, 128), BF),
            vmem((WIDE, 128, 128), BF),
            vmem((2, WIDE, 64, 128), F32),
            vmem((2, WIDE, 64, 128), F32),
            vmem((XB, 256, 128), F32),
            vmem((2, 48, 16, 128), F32),
            vmem((2, XB, 16, 256), BF),
            vmem((XB, 256, 128), BF),
            vmem((XB, 256, 128), BF),
            vmem((STEPS, 2, 8, 128, 128), BF),
            vmem((STEPS, 4, 128, 128), BF),
            vmem((STEPS, 2, 8, 128, 128), BF),
            vmem((STEPS, 2, 6, 128, 128), BF),
            vmem((NZ, XB, 128), BF),
            vmem((1, 128), F32),
            vmem((NZ * XB, 128), F32),
            vmem((128, 128), F32),
            dma((CAP,)),
            dma((NB,)),
            dma((NB,)),
            dma((NB,)),
            dma((NB,)),
            dma((STEPS, MOVES)),
            dma((STEPS, MOVES)),
            dma((NB,)),
            dma((NB,)),
            dma((NB,)),
            dma((NB,)),
            dma((2,)),
        ],
        compiler_params=params(56, collective_id=0, has_side_effects=True),
        name="deconvolve",
    )(slot_plane, shear_offsets, profile_z, profile_x, profile_y, raw_planes, dark_level.reshape(1, 128))
    return decode(coded, peaks)


def solution(mesh):
    in_specs = (P("gz", None, "gy"), P("gz"), P(), P(), P(), P(), P())
    out_specs = P("gz", None, "gy")
    return jax.shard_map(shards, mesh=mesh, in_specs=in_specs, out_specs=out_specs, check_vma=False)
```
